256 devices in a mesh: roll: 4 (over z_lo), seq: 16 (over y, x), tp: 4 (over z_hi, core).
Axes of the slice: x: 4, y: 4, z: 8 (z_hi: 2, z_lo: 4; z = z_hi * 4 + z_lo), core: 2. Of those that a mesh axis runs over, the one named last changes fastest.
Arguments:
- prompt_kv: bfloat16 [2, 256, 1024], P(None, ('roll', 'seq', 'tp')), may hold values from -6 to 6
- comp_q: bfloat16 [4, 2048, 8192], P('roll', 'seq', 'tp'), may hold values from -6 to 6
- comp_kv: bfloat16 [2, 4, 2048, 1024], P(None, 'roll', 'seq', 'tp'), may hold values from -6 to 6
- out_grad: bfloat16 [4, 2048, 8192], P('roll', 'seq', 'tp'), may hold values from -6 to 6
- lengths: int32 [4], P('roll'), may hold values from 256 to 2048, as said below
Outputs:
- attn_out: bfloat16 [4, 2048, 8192], P('roll', 'seq', 'tp')
- q_grad: bfloat16 [4, 2048, 8192], P('roll', 'seq', 'tp')
- comp_kv_grad: float32 [2, 4, 2048, 1024], P(None, 'roll', 'seq', 'tp')
- prompt_kv_grad: float32 [2, 256, 1024], P(None, ('roll', 'seq'), 'tp')
The draws below stay inside these ranges and needn't reach their ends.
Inputs may be any that keep to these rules, and one draw needn't show every extreme that they name: `lengths`: positions at or beyond a rollout's length are padding. In every draw one rollout uses all 2048 positions and one an eighth of them.
All inputs are finite; a program needn't handle non-finite values.
Results may differ from the reference program's by a relative error of at most 0.0088.
Values may be sent and summed in bfloat16 or wider, within the bound.
A program may use at most 64 MiB of HBM per device.

```python
import math
import jax
import jax.numpy as jnp
from jax import lax

H = 64
KVH = 8
HD = 128
P_SIZE = 256
C = 2048
ROLLOUTS = 4


def draw_prompt_kv(key, part):
    key = jax.random.fold_in(key, 11)
    base_draw = jnp.clip(jax.random.normal(key, (2, P_SIZE, KVH * HD), jnp.float32), -6.0, 6.0)
    return base_draw.astype(jnp.bfloat16)


def draw_comp_q(key, part):
    key = jax.random.fold_in(key, 21)
    base_draw = jnp.clip(jax.random.normal(key, (ROLLOUTS, C, H * HD), jnp.float32), -6.0, 6.0)
    return base_draw.astype(jnp.bfloat16)


def draw_lengths(key, part):
    key = jax.random.fold_in(key, 5)
    draw_key, rank_key = jax.random.split(key)
    values = jax.random.randint(draw_key, (ROLLOUTS,), C // 8, C + 1)
    ranking = jax.random.permutation(rank_key, ROLLOUTS)
    values = jnp.where(ranking == 0, C, values)
    values = jnp.where(ranking == 1, C // 8, values)
    return values.astype(jnp.int32)


def block_scale(key, extent, cuts, smallest, high):
    level, own = 1.0, jax.random.fold_in(key, 6)
    for dim, shards_of in cuts:
        heights = jnp.exp(jax.random.uniform(jax.random.fold_in(own, dim), (shards_of,), jnp.float32, smallest / len(cuts), high / len(cuts)))
        level = level * jnp.repeat(heights, extent[dim] // shards_of).reshape([-1 if axis == dim else 1 for axis in range(len(extent))])
    return level


def centred(own_key, extent, scale, limit, shards=(), kind=jnp.bfloat16):
    values = scale * jax.random.normal(own_key, extent, jnp.float32)
    if shards:
        values = values * block_scale(own_key, extent, shards, -0.22, 0.18)
    return jnp.clip(values, -limit, limit).astype(kind)


def setup_inputs(seed: int = 0) -> dict:
    key_of = jax.random.split(jax.random.key(seed), 6)
    return {
        "prompt_kv": draw_prompt_kv(jax.random.fold_in(key_of[5], 71), 0),
        "comp_q": draw_comp_q(jax.random.fold_in(key_of[5], 71), 0),
        "comp_kv": centred(key_of[2], (2, ROLLOUTS, C, KVH * HD), 1.0, 6.0, ((1, 4), (2, 16), (3, 4))),
        "out_grad": centred(key_of[3], (ROLLOUTS, C, H * HD), 1.0, 6.0, ((0, 4), (1, 16), (2, 4))),
        "lengths": draw_lengths(jax.random.fold_in(key_of[5], 71), 0),
    }


floor_score = -1e+30

def head_block(query_rows, cotangent_rows, prompt_pair, own_pair, length):
    score_scale = 1.0 / math.sqrt(HD)
    key_rows = jnp.concatenate([prompt_pair[0], own_pair[0]], axis=0).astype(jnp.float32)
    value_rows = jnp.concatenate([prompt_pair[1], own_pair[1]], axis=0).astype(jnp.float32)
    queries = query_rows.astype(jnp.float32)
    scores = jnp.einsum('gcd,nd->gcn', queries, key_rows, precision=lax.Precision.HIGHEST) * score_scale
    query_pos = jnp.arange(C, dtype=jnp.int32)
    key_pos = jnp.arange(P_SIZE + C, dtype=jnp.int32) - P_SIZE
    allowed = (key_pos[None, :] < 0) | (key_pos[None, :] <= query_pos[:, None]) & (key_pos[None, :] < length)
    scores = jnp.where(allowed[None], scores, floor_score)
    row_max = lax.optimization_barrier(jnp.max(scores, axis=-1, keepdims=True))
    raised = jnp.exp(scores - row_max)
    weights = raised / lax.optimization_barrier(jnp.sum(raised, axis=-1, keepdims=True))
    rounded = weights.astype(jnp.bfloat16)
    rounded_wide = rounded.astype(jnp.float32)
    mixed = jnp.einsum('gcn,nd->gcd', rounded_wide, value_rows, precision=lax.Precision.HIGHEST)
    live = (query_pos < length)[None, :, None]
    attn_out = jnp.where(live, mixed, 0.0).astype(jnp.bfloat16)
    grad_live = jnp.where(live, cotangent_rows, jnp.zeros_like(cotangent_rows))
    grad_wide = grad_live.astype(jnp.float32)
    row_delta = lax.optimization_barrier(jnp.sum(grad_wide * mixed, axis=-1, keepdims=True))
    weight_grad = jnp.einsum('gcd,nd->gcn', grad_wide, value_rows, precision=lax.Precision.HIGHEST)
    score_grad = (score_scale * weights * (weight_grad - row_delta)).astype(jnp.bfloat16)
    grad_scores = score_grad.astype(jnp.float32)
    query_grad = jnp.einsum('gcn,nd->gcd', grad_scores, key_rows, precision=lax.Precision.HIGHEST).astype(jnp.bfloat16)
    key_grad = jnp.einsum('gcn,gcd->nd', grad_scores, queries, precision=lax.Precision.HIGHEST)
    value_grad = jnp.einsum('gcn,gcd->nd', rounded_wide, grad_wide, precision=lax.Precision.HIGHEST)
    return (attn_out, query_grad, key_grad[:P_SIZE], value_grad[:P_SIZE], key_grad[P_SIZE:], value_grad[P_SIZE:])

def spread_heads(stacked):
    return stacked.transpose(1, 0, 2).reshape(stacked.shape[1], KVH * HD)

def query_heads_of(matrix):
    return matrix.reshape(C, KVH, H // KVH, HD).transpose(1, 2, 0, 3)

def reference(prompt_kv, comp_q, comp_kv, out_grad, lengths):
    prompt_split = prompt_kv.reshape(2, P_SIZE, KVH, HD).transpose(2, 0, 1, 3)
    out_list = []
    grad_list = []
    own_list = []
    prompt_total = jnp.zeros((2, P_SIZE, KVH * HD), jnp.float32)
    for rollout in range(ROLLOUTS):
        query_split = query_heads_of(comp_q[rollout])
        cotangent_split = query_heads_of(out_grad[rollout])
        own_split = comp_kv[:, rollout].reshape(2, C, KVH, HD).transpose(2, 0, 1, 3)
        length = lengths[rollout]

        def one_head(pieces):
            return head_block(pieces[0], pieces[1], pieces[2], pieces[3], length)
        results = lax.map(one_head, (query_split, cotangent_split, prompt_split, own_split))
        out_list.append(results[0].transpose(2, 0, 1, 3).reshape(C, H * HD))
        grad_list.append(results[1].transpose(2, 0, 1, 3).reshape(C, H * HD))
        prompt_total = prompt_total + jnp.stack([spread_heads(results[2]), spread_heads(results[3])])
        own_list.append(jnp.stack([spread_heads(results[4]), spread_heads(results[5])]))
    return (jnp.stack(out_list), jnp.stack(grad_list), jnp.stack(own_list, axis=1), prompt_total)
```

```python
import math

import jax
import jax.numpy as jnp
from jax import lax
from jax.experimental import pallas as pl
from jax.experimental.pallas import tpu as pltpu
from jax.sharding import PartitionSpec as P

HD = 128
BLOCK = 128
GROUP = 8
ROWS = GROUP * BLOCK
SLAB = 4 * BLOCK
PROMPT = 256
SCALE = 1.0 / math.sqrt(HD)
LOG2_SCALE = SCALE * math.log2(math.e)
FLOOR = -1e30
f32 = jnp.float32
bf16 = jnp.bfloat16
MESH = pl.DeviceIdType.MESH


def dot_nt(a, b):
    return lax.dot_general(a, b, (((1,), (1,)), ((), ())), preferred_element_type=f32)


def dot_nn(a, b):
    return lax.dot_general(a, b, (((1,), (0,)), ((), ())), preferred_element_type=f32)


def eye(n):
    rows = lax.broadcasted_iota(jnp.int32, (n, n), 0)
    cols = lax.broadcasted_iota(jnp.int32, (n, n), 1)
    return jnp.where(rows == cols, 1.0, 0.0).astype(bf16)


def rem4(i):
    return lax.rem(i, 4)


def rem16(i):
    return lax.rem(i, 16)


def kernel(
    len_ref, pk_ref, q_ref, kv_ref, do_ref,
    out_ref, qg_ref, okv_ref, opk_ref,
    qs, dos, kvb, pb, pp, mc, mx, sm, o_t, dq_t, dl, acc,
    ds_part, own, m1, m2, tot, tsend, n1, n2,
    buf_a, buf_a2, buf_b, pgs, rec_c, src_d, rec_d,
    s1, r1, s2, r2, sm1, rm1, sm2, rm2, sn1, rn1, sn2, rn2,
    s_a, r_a, s_b, r_b, s_c, r_c, s_d, r_d,
):
    roll = lax.axis_index("roll")
    seq = lax.axis_index("seq")
    tp = lax.axis_index("tp")
    y = lax.div(seq, 4)
    x = rem4(seq)
    col = roll * 4 + tp
    length = len_ref[0]

    def x_dev(d):
        return {"seq": y * 4 + rem4(x + d)}

    def y_dev(d):
        return {"seq": rem4(y + d) * 4 + x}

    def seq_dev(d):
        return {"seq": rem16(seq + d)}

    def col_dev(d):
        c = rem16(col + d)
        return {"roll": lax.div(c, 4), "tp": rem4(c)}

    def inner(g, d):
        return x_dev(d) if g == 0 else y_dev(d)

    def outer(g, d):
        return y_dev(d) if g == 0 else x_dev(d)

    def slab_of(g):
        return y if g == 0 else x

    def block_of(g):
        return x if g == 0 else y

    def rcopy(src, dst, ssem, rsem, dev):
        return pltpu.make_async_remote_copy(
            src_ref=src, dst_ref=dst, send_sem=ssem, recv_sem=rsem, device_id=dev, device_id_type=MESH
        )

    def rows_of(b):
        return pl.ds(pl.multiple_of(b * BLOCK, BLOCK), BLOCK)

    barrier = pltpu.get_barrier_semaphore()

    @pl.loop(1, 16)
    def _(d):
        pl.semaphore_signal(barrier, inc=1, device_id=seq_dev(d), device_id_type=MESH)
        pl.semaphore_signal(barrier, inc=1, device_id=col_dev(d), device_id_type=MESH)

    for g in range(2):
        for kv in range(2):
            kvb[g, slab_of(g), kv, rows_of(block_of(g)), :] = kv_ref[kv, :, g * HD : (g + 1) * HD]
    buf_a[pl.ds(pl.multiple_of(col * 8, 8), 8), :] = pk_ref[tp]

    pl.semaphore_wait(barrier, 30)

    def block_send(g, k):
        o, b = slab_of(g), block_of(g)
        if k == 0:
            ref, d = kvb.at[g, o, :, rows_of(b), :], 1
        elif k == 1:
            ref, d = kvb.at[g, o, :, rows_of(b), :], 3
        elif k == 2:
            ref, d = kvb.at[g, o, 0, rows_of(rem4(b + 3)), :], 1
        else:
            ref, d = kvb.at[g, o, 1, rows_of(rem4(b + 1)), :], 3
        return rcopy(ref, ref, s1.at[g, k], r1.at[g, k], inner(g, d))

    def block_recv(g, k):
        o, b = slab_of(g), block_of(g)
        if k == 0:
            ref = kvb.at[g, o, :, rows_of(rem4(b + 3)), :]
        elif k == 1:
            ref = kvb.at[g, o, :, rows_of(rem4(b + 1)), :]
        elif k == 2:
            ref = kvb.at[g, o, 0, rows_of(rem4(b + 2)), :]
        else:
            ref = kvb.at[g, o, 1, rows_of(rem4(b + 2)), :]
        return rcopy(ref, ref, s1.at[g, k], r1.at[g, k], inner(g, 1))

    def slab_send(g, k):
        o = slab_of(g)
        if k == 0:
            ref, d = kvb.at[g, o], 1
        elif k == 1:
            ref, d = kvb.at[g, o], 3
        elif k == 2:
            ref, d = kvb.at[g, rem4(o + 3), 0], 1
        else:
            ref, d = kvb.at[g, rem4(o + 1), 1], 3
        return rcopy(ref, ref, s2.at[g, k], r2.at[g, k], outer(g, d))

    def slab_recv(g, k):
        o = slab_of(g)
        if k == 0:
            ref = kvb.at[g, rem4(o + 3)]
        elif k == 1:
            ref = kvb.at[g, rem4(o + 1)]
        else:
            ref = kvb.at[g, rem4(o + 2), k - 2]
        return rcopy(ref, ref, s2.at[g, k], r2.at[g, k], outer(g, 1))

    def a_send(d):
        dev = col_dev(d)
        dst = buf_a.at[pl.ds(pl.multiple_of(col * 8, 8), 8), :]
        return rcopy(pk_ref.at[dev["tp"]], dst, s_a.at[d], r_a.at[d], dev)

    def a_recv(d):
        c = rem16(col + 16 - d)
        ref = buf_a.at[pl.ds(pl.multiple_of(c * 8, 8), 8), :]
        return rcopy(pk_ref.at[tp], ref, s_a.at[d], r_a.at[d], col_dev(d))

    def seq_rows(s):
        return pl.ds(pl.multiple_of(s * 16, 16), 16)

    def b_send(d):
        return rcopy(buf_a2, buf_b.at[:, seq_rows(seq), :], s_b.at[d], r_b.at[d], seq_dev(d))

    def b_recv(d):
        s = rem16(seq + 16 - d)
        return rcopy(buf_a2, buf_b.at[:, seq_rows(s), :], s_b.at[d], r_b.at[d], seq_dev(d))

    def c_send(d):
        s = rem16(seq + d)
        return rcopy(pgs.at[:, seq_rows(s), :], rec_c.at[seq], s_c.at[d], r_c.at[d], seq_dev(d))

    def c_recv(d):
        s = rem16(seq + 16 - d)
        return rcopy(rec_c.at[s], rec_c.at[s], s_c.at[d], r_c.at[d], seq_dev(d))

    def d_send(d):
        r = rem4(roll + d)
        return rcopy(src_d.at[r], rec_d.at[roll], s_d.at[d], r_d.at[d], {"roll": r})

    def d_recv(d):
        r = rem4(roll + 4 - d)
        return rcopy(rec_d.at[r], rec_d.at[r], s_d.at[d], r_d.at[d], {"roll": r})

    for k in range(2):
        for g in range(2):
            block_send(g, k).start()

    @pl.loop(1, 16)
    def _(d):
        a_send(d).start()

    live_rows = seq * BLOCK + lax.broadcasted_iota(jnp.int32, (BLOCK, HD), 0) < length
    for g in range(2):
        for h in range(GROUP):
            cols = slice((g * GROUP + h) * HD, (g * GROUP + h + 1) * HD)
            rows = slice(h * BLOCK, (h + 1) * BLOCK)
            qs[g, rows, :] = q_ref[:, cols]
            dos[g, rows, :] = jnp.where(live_rows, do_ref[:, cols].astype(f32), 0.0).astype(bf16)
    mx[...] = jnp.full(mx.shape, FLOOR, f32)
    sm[...] = jnp.zeros(sm.shape, f32)
    o_t[...] = jnp.zeros(o_t.shape, f32)
    dq_t[...] = jnp.zeros(dq_t.shape, f32)

    for g in range(2):
        block_recv(g, 0).wait_recv()
        block_send(g, 2).start()
        block_recv(g, 1).wait_recv()
        block_send(g, 3).start()

    @pl.loop(1, 16)
    def _(d):
        a_recv(d).wait_recv()

    for j in range(4):
        buf_a2[j] = buf_a[pl.ds(j, 16, stride=8), :].astype(bf16)

    @pl.loop(1, 16)
    def _(d):
        b_send(d).start()

    buf_b[:, seq_rows(seq), :] = buf_a2[...]

    for g in range(2):
        block_recv(g, 2).wait_recv()
        block_recv(g, 3).wait_recv()
        slab_send(g, 0).start()
        slab_send(g, 1).start()

    def fwd(g, c, k, v, p_ref, mask):
        n = k.shape[0]
        v_t = dot_nt(eye(HD), v).astype(bf16)
        s = dot_nt(k, qs[g]) * LOG2_SCALE
        if mask is not None:
            s = jnp.where(mask(n), s, FLOOR)
        m_old = mx[g]
        m_new = jnp.maximum(m_old, jnp.max(s, axis=0, keepdims=True))
        p = jnp.exp2(s - m_new)
        alpha = jnp.exp2(m_old - m_new)
        mx[g] = m_new
        mc[g, c] = m_new
        sm[g] = sm[g] * alpha + jnp.sum(p, axis=0, keepdims=True)
        rounded = p.astype(bf16)
        p_ref[...] = rounded
        o_t[g] = o_t[g] * alpha + dot_nn(v_t, rounded)

    def pick(g):
        return jnp.where(g == 0, y, x)

    def offset(kind):
        return jnp.where(kind == 2, 1, jnp.where(kind == 3, 3, jnp.where(kind == 4, 2, 0)))

    def fwd_slab(g, slab):
        all_seen = jnp.where(g == 0, slab < y, (y == 3) & (slab < x))
        none_seen = (g == 0) & (slab > y)

        def mask(n):
            row = lax.broadcasted_iota(jnp.int32, (n, 1), 0)
            block = lax.div(row, BLOCK)
            key_block = jnp.where(g == 0, slab * 4 + block, block * 4 + slab)
            key_pos = key_block * BLOCK + lax.rem(row, BLOCK)
            lane = lax.broadcasted_iota(jnp.int32, (1, ROWS), 1)
            return key_pos <= seq * BLOCK + lax.rem(lane, BLOCK)

        @pl.when(all_seen)
        def _():
            fwd(g, slab, kvb[g, slab, 0], kvb[g, slab, 1], pb.at[g, slab], None)

        @pl.when(jnp.logical_not(all_seen | none_seen))
        def _():
            fwd(g, slab, kvb[g, slab, 0], kvb[g, slab, 1], pb.at[g, slab], mask)

    @pl.loop(0, 10)
    def _(i):
        g = lax.rem(i, 2)
        kind = lax.div(i, 2)

        @pl.when(i == 2)
        def _():
            @pl.loop(1, 16)
            def _(d):
                b_recv(d).wait_recv()

        @pl.when(i == 4)
        def _():
            for h in range(2):
                slab_recv(h, 0).wait_recv()
                slab_send(h, 2).start()
                slab_recv(h, 1).wait_recv()
                slab_send(h, 3).start()

        @pl.when(i == 8)
        def _():
            for h in range(2):
                slab_recv(h, 2).wait_recv()
                slab_recv(h, 3).wait_recv()

        @pl.when(kind == 1)
        def _():
            fwd(g, 4, buf_b[g], buf_b[2 + g], pp.at[g], None)

        @pl.when(kind != 1)
        def _():
            fwd_slab(g, rem4(pick(g) + offset(kind)))

    @pl.loop(0, 2)
    def _(g):
        inv = 1.0 / sm[g]
        mixed = o_t[g] * inv
        dl[g] = jnp.sum(dot_nt(eye(HD), dos[g]) * mixed, axis=0, keepdims=True)
        sm[g] = inv
        lane = lax.broadcasted_iota(jnp.int32, (1, ROWS), 1)
        live = seq * BLOCK + lax.rem(lane, BLOCK) < length
        rounded = jnp.where(live, mixed, 0.0).astype(bf16)
        for h in range(GROUP):
            head = dot_nt(eye(BLOCK), rounded[:, h * BLOCK : (h + 1) * BLOCK])
            out_ref[:, pl.ds(pl.multiple_of((g * GROUP + h) * HD, HD), HD)] = head.astype(bf16)

    def bwd(g, c, k, v, p):
        n = k.shape[0]
        k_t = dot_nt(eye(HD), k).astype(bf16)
        factor = jnp.exp2(mc[g, c] - mx[g]) * sm[g]
        dp = dot_nt(v, dos[g])
        w = p.astype(f32) * factor
        ds = (w * (dp - dl[g])).astype(bf16)
        acc[1, :n] = dot_nn(w.astype(bf16), dos[g])
        acc[0, :n] = dot_nn(ds, qs[g]) * SCALE
        dq_t[g] += dot_nn(k_t, ds)

    def order(kind):
        return jnp.where(kind == 0, 2, jnp.where(kind == 1, 1, jnp.where(kind == 2, 3, 0)))

    def m1_send(g, kv):
        return rcopy(ds_part.at[g, 0, kv], m1.at[g, kv], sm1.at[g, kv], rm1.at[g, kv], outer(g, 1 if kv == 0 else 3))

    def m2_send(g, k):
        return rcopy(ds_part.at[g, 1 + k], m2.at[g, k], sm2.at[g, k], rm2.at[g, k], outer(g, 1 if k == 0 else 3))

    @pl.loop(0, 10)
    def _(i):
        g = lax.rem(i, 2)
        kind = lax.div(i, 2)
        slab = rem4(pick(g) + order(kind))
        none_seen = (g == 0) & (slab > y)

        @pl.when(kind == 3)
        def _():
            bwd(g, 4, buf_b[g], buf_b[2 + g], pp[g])
            pgs[g] = acc[0, :PROMPT].astype(bf16)
            pgs[2 + g] = acc[1, :PROMPT].astype(bf16)

        @pl.when((kind != 3) & jnp.logical_not(none_seen))
        def _():
            bwd(g, slab, kvb[g, slab, 0], kvb[g, slab, 1], pb[g, slab])

        @pl.when(none_seen & (kind != 3))
        def _():
            acc[...] = jnp.zeros(acc.shape, f32)

        @pl.when(kind < 3)
        def _():
            ds_part[g, kind] = acc[...].astype(bf16)

        @pl.when(kind == 4)
        def _():
            own[g] = acc[...]

        for h in range(2):

            @pl.when(i == h)
            def _():
                m1_send(h, 0).start()
                m1_send(h, 1).start()

            @pl.when(i == 2 + h)
            def _():
                m1_send(h, 0).wait_recv()
                ds_part[h, 1, 0] = (acc[0] + m1[h, 0].astype(f32)).astype(bf16)
                m2_send(h, 0).start()

            @pl.when(i == 4 + h)
            def _():
                m1_send(h, 1).wait_recv()
                ds_part[h, 2, 1] = (acc[1] + m1[h, 1].astype(f32)).astype(bf16)
                m2_send(h, 1).start()

        @pl.when(i == 7)
        def _():
            rec_c[seq] = pgs[:, seq_rows(seq), :]

            @pl.loop(1, 16)
            def _(d):
                c_send(d).start()

    @pl.loop(0, 2)
    def _(g):
        rounded = (dq_t[g] * SCALE).astype(bf16)
        for h in range(GROUP):
            head = dot_nt(eye(BLOCK), rounded[:, h * BLOCK : (h + 1) * BLOCK])
            qg_ref[:, pl.ds(pl.multiple_of((g * GROUP + h) * HD, HD), HD)] = head.astype(bf16)

    def n1_send(g, kv):
        return rcopy(tsend.at[g, 0, kv], n1.at[g, kv], sn1.at[g, kv], rn1.at[g, kv], inner(g, 1 if kv == 0 else 3))

    def n2_send(g, k):
        return rcopy(tsend.at[g, 1 + k], n2.at[g, k], sn2.at[g, k], rn2.at[g, k], inner(g, 1 if k == 0 else 3))

    for g in range(2):
        b = block_of(g)
        m2_send(g, 0).wait_recv()
        m2_send(g, 1).wait_recv()
        tot[g] = own[g] + m2[g, 0].astype(f32) + m2[g, 1].astype(f32)
        tsend[g, 0] = tot[g, :, rows_of(rem4(b + 2)), :].astype(bf16)
        n1_send(g, 0).start()
        n1_send(g, 1).start()

    @pl.loop(1, 16)
    def _(d):
        c_recv(d).wait_recv()

    total_c = rec_c[0].astype(f32)
    for s in range(1, 16):
        total_c = total_c + rec_c[s].astype(f32)
    for r in range(4):
        part = total_c[:, r * 4 : (r + 1) * 4, :]
        src_d[r] = jnp.concatenate([part, jnp.zeros_like(part)], axis=1)
    for d in range(1, 4):
        d_send(d).start()
    rec_d[roll] = src_d[roll]

    for g in range(2):
        b = block_of(g)
        n1_send(g, 0).wait_recv()
        n1_send(g, 1).wait_recv()
        right = rows_of(rem4(b + 1))
        left = rows_of(rem4(b + 3))
        tsend[g, 1, 0] = (tot[g, 0, right, :] + n1[g, 0].astype(f32)).astype(bf16)
        tsend[g, 1, 1] = tot[g, 1, right, :].astype(bf16)
        tsend[g, 2, 0] = tot[g, 0, left, :].astype(bf16)
        tsend[g, 2, 1] = (tot[g, 1, left, :] + n1[g, 1].astype(f32)).astype(bf16)
        n2_send(g, 0).start()
        n2_send(g, 1).start()

    for d in range(1, 4):
        d_recv(d).wait_recv()
    total_d = rec_d[0] + rec_d[1] + rec_d[2] + rec_d[3]
    for g in range(2):
        for kv in range(2):
            opk_ref[kv, :, g * HD : (g + 1) * HD] = total_d[kv * 2 + g, 0:4, :]

    for g in range(2):
        b = block_of(g)
        n2_send(g, 0).wait_recv()
        n2_send(g, 1).wait_recv()
        for kv in range(2):
            okv_ref[kv, :, g * HD : (g + 1) * HD] = (
                tot[g, kv, rows_of(b), :] + n2[g, 0, kv].astype(f32) + n2[g, 1, kv].astype(f32)
            )

    for g in range(2):
        for k in range(4):
            block_send(g, k).wait_send()
            slab_send(g, k).wait_send()
        for k in range(2):
            m1_send(g, k).wait_send()
            m2_send(g, k).wait_send()
            n1_send(g, k).wait_send()
            n2_send(g, k).wait_send()

    @pl.loop(1, 16)
    def _(d):
        a_send(d).wait_send()
        b_send(d).wait_send()
        c_send(d).wait_send()

    for d in range(1, 4):
        d_send(d).wait_send()


def shards(prompt_kv, comp_q, comp_kv, out_grad, lengths):
    pieces = prompt_kv.reshape(2, 4, 2, HD).transpose(1, 0, 2, 3).reshape(4, 4, HD).astype(f32)
    pieces = jnp.pad(pieces, ((0, 0), (0, 4), (0, 0)))
    vmem = pl.BlockSpec(memory_space=pltpu.VMEM)
    dma = pltpu.SemaphoreType.DMA
    width = comp_q.shape[2]
    out, q_grad, own_grad, prompt_grad = pl.pallas_call(
        kernel,
        out_shape=(
            jax.ShapeDtypeStruct((BLOCK, width), bf16),
            jax.ShapeDtypeStruct((BLOCK, width), bf16),
            jax.ShapeDtypeStruct((2, BLOCK, 2 * HD), f32),
            jax.ShapeDtypeStruct((2, 4, 2 * HD), f32),
        ),
        in_specs=[pl.BlockSpec(memory_space=pltpu.SMEM)] + [vmem] * 4,
        out_specs=[vmem] * 4,
        scratch_shapes=[
            pltpu.VMEM((2, ROWS, HD), bf16),
            pltpu.VMEM((2, ROWS, HD), bf16),
            pltpu.VMEM((2, 4, 2, SLAB, HD), bf16),
            pltpu.VMEM((2, 4, SLAB, ROWS), bf16),
            pltpu.VMEM((2, PROMPT, ROWS), bf16),
            pltpu.VMEM((2, 5, 1, ROWS), f32),
            pltpu.VMEM((2, 1, ROWS), f32),
            pltpu.VMEM((2, 1, ROWS), f32),
            pltpu.VMEM((2, HD, ROWS), f32),
            pltpu.VMEM((2, HD, ROWS), f32),
            pltpu.VMEM((2, 1, ROWS), f32),
            pltpu.VMEM((2, SLAB, HD), f32),
            pltpu.VMEM((2, 3, 2, SLAB, HD), bf16),
            pltpu.VMEM((2, 2, SLAB, HD), f32),
            pltpu.VMEM((2, 2, SLAB, HD), bf16),
            pltpu.VMEM((2, 2, 2, SLAB, HD), bf16),
            pltpu.VMEM((2, 2, SLAB, HD), f32),
            pltpu.VMEM((2, 3, 2, BLOCK, HD), bf16),
            pltpu.VMEM((2, 2, BLOCK, HD), bf16),
            pltpu.VMEM((2, 2, 2, BLOCK, HD), bf16),
            pltpu.VMEM((16 * 8, HD), f32),
            pltpu.VMEM((4, 16, HD), bf16),
            pltpu.VMEM((4, PROMPT, HD), bf16),
            pltpu.VMEM((4, PROMPT, HD), bf16),
            pltpu.VMEM((16, 4, 16, HD), bf16),
            pltpu.VMEM((4, 4, 8, HD), f32),
            pltpu.VMEM((4, 4, 8, HD), f32),
        ]
        + [dma((2, 4))] * 4
        + [dma((2, 2))] * 8
        + [dma((16,))] * 6
        + [dma((4,))] * 2,
        compiler_params=pltpu.CompilerParams(
            collective_id=0, has_side_effects=True, vmem_limit_bytes=56 * 2**20
        ),
    )(lengths, pieces, comp_q[0], comp_kv[:, 0], out_grad[0])
    return out[None], q_grad[None], own_grad[:, None], prompt_grad


def solution(mesh):
    in_specs = (
        P(None, ("roll", "seq", "tp"), None),
        P("roll", "seq", "tp"),
        P(None, "roll", "seq", "tp"),
        P("roll", "seq", "tp"),
        P("roll"),
    )
    out_specs = (
        P("roll", "seq", "tp"),
        P("roll", "seq", "tp"),
        P(None, "roll", "seq", "tp"),
        P(None, ("roll", "seq"), "tp"),
    )
    return jax.shard_map(shards, mesh=mesh, in_specs=in_specs, out_specs=out_specs, check_vma=False)
```

```python
import math

import jax
import jax.numpy as jnp
from jax import lax
from jax.experimental import pallas as pl
from jax.experimental.pallas import tpu as pltpu
from jax.sharding import PartitionSpec as P

HD = 128
BLOCK = 128
GROUP = 8
ROWS = GROUP * BLOCK
SLAB = 4 * BLOCK
PROMPT = 256
SCALE = 1.0 / math.sqrt(HD)
LOG2_SCALE = SCALE * math.log2(math.e)
FLOOR = -1e30
f32 = jnp.float32
bf16 = jnp.bfloat16
MESH = pl.DeviceIdType.MESH


def dot_nt(a, b):
    return lax.dot_general(a, b, (((1,), (1,)), ((), ())), preferred_element_type=f32)


def dot_nn(a, b):
    return lax.dot_general(a, b, (((1,), (0,)), ((), ())), preferred_element_type=f32)


def eye(n):
    rows = lax.broadcasted_iota(jnp.int32, (n, n), 0)
    cols = lax.broadcasted_iota(jnp.int32, (n, n), 1)
    return jnp.where(rows == cols, 1.0, 0.0).astype(bf16)


def rem4(i):
    return lax.rem(i, 4)


def kernel(
    len_ref, pk_ref, q_hbm, kv_hbm, do_hbm,
    out_hbm, qg_hbm, okv_hbm, opk_hbm,
    q_ref, kv_ref, do_ref, out_ref, qg_ref, okv_ref, opk_ref,
    qs, dos, kvb, pb, pp, mc, mx, sm, o_t, dq_t, dl, acc,
    part, own, tot, irec, osend, orec,
    buf_s, buf_p, buf_b, pgs, rec_r, src_y, rec_y, src_x, rec_x,
    s_in, r_in, s_out, r_out, s_ri, r_ri, s_ro, r_ro,
    s_p, r_p, s_c, r_c, s_io,
):
    roll = lax.axis_index("roll")
    seq = lax.axis_index("seq")
    tp = lax.axis_index("tp")
    y = lax.div(seq, 4)
    x = rem4(seq)
    length = len_ref[0]
    steps = (1, 3, 2)

    def x_dev(d):
        return {"seq": y * 4 + rem4(x + d)}

    def y_dev(d):
        return {"seq": rem4(y + d) * 4 + x}

    def roll_dev(d):
        return {"roll": rem4(roll + d)}

    def tp_dev(d):
        return {"tp": rem4(tp + d)}

    def inner(g, d):
        return x_dev(d) if g == 0 else y_dev(d)

    def outer(g, d):
        return y_dev(d) if g == 0 else x_dev(d)

    def rcopy(src, dst, ssem, rsem, dev):
        return pltpu.make_async_remote_copy(
            src_ref=src, dst_ref=dst, send_sem=ssem, recv_sem=rsem, device_id=dev, device_id_type=MESH
        )

    def span(i, n):
        return pl.ds(pl.multiple_of(i * n, n), n)

    barrier = pltpu.get_barrier_semaphore()
    for line in (tp_dev, roll_dev, y_dev, x_dev):
        for d in (2, 1, 3):
            pl.semaphore_signal(barrier, inc=1, device_id=line(d), device_id_type=MESH)
    kv_in = pltpu.make_async_copy(kv_hbm, kv_ref, s_io.at[0])
    q_in = pltpu.make_async_copy(q_hbm, q_ref, s_io.at[1])
    do_in = pltpu.make_async_copy(do_hbm, do_ref, s_io.at[2])
    kv_in.start()
    q_in.start()
    do_in.start()

    prompt_row = pk_ref[...].astype(f32)
    pieces = [prompt_row[:, t * HD : (t + 1) * HD] for t in range(8)]
    buf_s[span(seq, 16), :] = jnp.concatenate(pieces, axis=0)
    kv_in.wait()
    for g in range(2):
        for kv in range(2):
            kvb[g, 0, kv, :BLOCK, :] = kv_ref[kv, :, g * HD : (g + 1) * HD]

    for p in range(1, 4):

        @pl.when(y + p < 4)
        def _():
            kvb[1, :, :, p * BLOCK : (p + 1) * BLOCK, :] = jnp.zeros((4, 2, BLOCK, HD), bf16)

    pl.semaphore_wait(barrier, 12)

    def seen_slab(g, e, act):
        if g == 0 and e > 0:
            pl.when(y + e >= 4)(act)
        else:
            act()

    def outer_copy(g, k):
        d = steps[k]
        src = kvb.at[g, 0, :, :BLOCK, :]
        return rcopy(src, kvb.at[g, 4 - d, :, :BLOCK, :], s_out.at[g, k], r_out.at[g, k], outer(g, d))

    def outer_start(g, k):
        def act():
            outer_copy(g, k).start()

        pl.when(y + steps[k] < 4)(act) if g == 0 else act()

    def inner_copy(g, e, k):
        d = steps[k]
        src = kvb.at[g, e, :, :BLOCK, :]
        dst = kvb.at[g, e, :, (4 - d) * BLOCK : (5 - d) * BLOCK, :]
        return rcopy(src, dst, s_in.at[g, e, k], r_in.at[g, e, k], inner(g, d))

    def inner_do(g, e, sends, act):
        def each():
            for k in range(3):
                if g == 0:
                    act(k)
                else:
                    pl.when(y + steps[k] < 4 if sends else y >= steps[k])(lambda: act(k))

        seen_slab(g, e, each)

    def inner_start(g, e):
        inner_do(g, e, True, lambda k: inner_copy(g, e, k).start())

    def inner_wait(g, e):
        inner_do(g, e, False, lambda k: inner_copy(g, e, k).wait_recv())

    def px_copy(k, from_offset):
        ref = buf_s.at[span(y * 4 + rem4(x + from_offset), 16), :]
        return rcopy(ref, ref, s_p.at[0, k], r_p.at[0, k], x_dev(steps[k]))

    def py_copy(k, from_offset):
        ref = buf_s.at[span(rem4(y + from_offset), 64), :]
        return rcopy(ref, ref, s_p.at[1, k], r_p.at[1, k], y_dev(steps[k]))

    def tp_copy(k, from_offset):
        dst = buf_b.at[:, span(roll * 4 + rem4(tp + from_offset), 16), :]
        return rcopy(buf_p.at[rem4(tp + steps[k])], dst, s_p.at[2, k], r_p.at[2, k], tp_dev(steps[k]))

    def roll_copy(k, from_offset):
        ref = buf_b.at[:, span(rem4(roll + from_offset), 64), :]
        return rcopy(ref, ref, s_p.at[3, k], r_p.at[3, k], roll_dev(steps[k]))

    prompt_copies = (px_copy, py_copy, tp_copy, roll_copy)

    def prompt_start(stage):
        for k in range(3):
            prompt_copies[stage](k, 0).start()

    def prompt_wait(stage):
        for k in range(3):
            prompt_copies[stage](k, 4 - steps[k]).wait_recv()

    for k in range(3):
        for g in range(2):
            outer_start(g, k)
    prompt_start(0)
    for g in range(2):
        inner_start(g, 0)

    q_in.wait()
    do_in.wait()
    live_rows = seq * BLOCK + lax.broadcasted_iota(jnp.int32, (BLOCK, HD), 0) < length
    for g in range(2):
        for h in range(GROUP):
            cols = slice((g * GROUP + h) * HD, (g * GROUP + h + 1) * HD)
            rows = slice(h * BLOCK, (h + 1) * BLOCK)
            qs[g, rows, :] = q_ref[:, cols]
            dos[g, rows, :] = jnp.where(live_rows, do_ref[:, cols].astype(f32), 0.0).astype(bf16)
    mx[...] = jnp.full(mx.shape, FLOOR, f32)
    sm[...] = jnp.zeros(sm.shape, f32)
    o_t[...] = jnp.zeros(o_t.shape, f32)
    dq_t[...] = jnp.zeros(dq_t.shape, f32)

    prompt_wait(0)
    prompt_start(1)
    for k in range(3):
        for g in range(2):
            e = 4 - steps[k]
            seen_slab(g, e, lambda: outer_copy(g, k).wait_recv())
            inner_start(g, e)

    def fwd(g, c, k, v, p_ref, mask):
        n = k.shape[0]
        v_t = dot_nt(eye(HD), v).astype(bf16)
        s = dot_nt(k, qs[g]) * LOG2_SCALE
        if mask is not None:
            s = jnp.where(mask(n), s, FLOOR)
        m_old = mx[g]
        m_new = jnp.maximum(m_old, jnp.max(s, axis=0, keepdims=True))
        p = jnp.exp2(s - m_new)
        alpha = jnp.exp2(m_old - m_new)
        mx[g] = m_new
        mc[g, c] = m_new
        sm[g] = sm[g] * alpha + jnp.sum(p, axis=0, keepdims=True)
        rounded = p.astype(bf16)
        p_ref[...] = rounded
        o_t[g] = o_t[g] * alpha + dot_nn(v_t, rounded)

    def fwd_slab(g, e):
        none_seen = (g == 0) & (e > 0) & (y + e < 4)
        all_seen = jnp.where(g == 0, y + e >= 4, (y == 3) & (x + e >= 4))

        def mask(n):
            row = lax.broadcasted_iota(jnp.int32, (n, 1), 0)
            block = lax.div(row, BLOCK)
            key_y = rem4(y + jnp.where(g == 0, e, block))
            key_x = rem4(x + jnp.where(g == 0, block, e))
            key_block = key_y * 4 + key_x
            key_pos = key_block * BLOCK + lax.rem(row, BLOCK)
            lane = lax.broadcasted_iota(jnp.int32, (1, ROWS), 1)
            return key_pos <= seq * BLOCK + lax.rem(lane, BLOCK)

        @pl.when(all_seen)
        def _():
            fwd(g, e, kvb[g, e, 0], kvb[g, e, 1], pb.at[g, e], None)

        @pl.when(jnp.logical_not(all_seen | none_seen))
        def _():
            fwd(g, e, kvb[g, e, 0], kvb[g, e, 1], pb.at[g, e], mask)

    @pl.loop(0, 10)
    def _(i):
        g = lax.rem(i, 2)
        kind = lax.div(i, 2)

        for h in range(2):
            for k, e in enumerate((0, 3, 1, 2)):

                @pl.when(i == 2 * k + h)
                def _():
                    inner_wait(h, e)

        @pl.when(i == 2)
        def _():
            prompt_wait(1)
            for t in range(4):
                for j in range(4):
                    buf_p[t, j] = buf_s[pl.ds(t * 4 + j, 16, stride=16), :].astype(bf16)
            prompt_start(2)
            buf_b[:, span(roll * 4 + tp, 16), :] = buf_p[tp]

        @pl.when(i == 5)
        def _():
            prompt_wait(2)
            prompt_start(3)

        @pl.when(i == 8)
        def _():
            prompt_wait(3)

        @pl.when(kind == 4)
        def _():
            fwd(g, 4, buf_b[g * 2], buf_b[g * 2 + 1], pp.at[g], None)

        @pl.when(kind != 4)
        def _():
            fwd_slab(g, jnp.where(kind == 1, 3, jnp.where(kind == 2, 1, jnp.where(kind == 3, 2, 0))))

    @pl.loop(0, 2)
    def _(g):
        inv = 1.0 / sm[g]
        mixed = o_t[g] * inv
        dl[g] = jnp.sum(dot_nt(eye(HD), dos[g]) * mixed, axis=0, keepdims=True)
        sm[g] = inv
        lane = lax.broadcasted_iota(jnp.int32, (1, ROWS), 1)
        live = seq * BLOCK + lax.rem(lane, BLOCK) < length
        rounded = jnp.where(live, mixed, 0.0).astype(bf16)
        for h in range(GROUP):
            head = dot_nt(eye(BLOCK), rounded[:, h * BLOCK : (h + 1) * BLOCK])
            out_ref[:, span(g * GROUP + h, HD)] = head.astype(bf16)

    out_done = pltpu.make_async_copy(out_ref, out_hbm, s_io.at[3])
    out_done.start()

    def bwd(g, c, k, v, p):
        n = k.shape[0]
        k_t = dot_nt(eye(HD), k).astype(bf16)
        factor = jnp.exp2(mc[g, c] - mx[g]) * sm[g]
        dp = dot_nt(v, dos[g])
        w = p.astype(f32) * factor
        ds = (w * (dp - dl[g])).astype(bf16)
        acc[1, :n] = dot_nn(w.astype(bf16), dos[g])
        acc[0, :n] = dot_nn(ds, qs[g]) * SCALE
        dq_t[g] += dot_nn(k_t, ds)

    def ri_copy(g, e, k):
        d = steps[k]
        src = part.at[g, e, :, d * BLOCK : (d + 1) * BLOCK, :]
        return rcopy(src, irec.at[g, e, k], s_ri.at[g, e, k], r_ri.at[g, e, k], inner(g, d))

    def ri_do(g, e, sends, act):
        def each():
            for k in range(3):
                if g == 0:
                    act(k)
                else:
                    pl.when(y + steps[k] >= 4 if sends else y < steps[k])(lambda: act(k))

        seen_slab(g, e, each)

    def ri_start(g, e):
        ri_do(g, e, True, lambda k: ri_copy(g, e, k).start())

    def ro_copy(g, e):
        return rcopy(osend.at[g, e], orec.at[g, e], s_ro.at[g, e], r_ro.at[g, e], outer(g, e))

    def ro_start(g, e):
        def act():
            own[g] = part[g, e, :, :BLOCK, :].astype(f32)

            def add(k):
                ri_copy(g, e, k).wait_recv()
                own[g] += irec[g, e, k].astype(f32)

            ri_do(g, e, False, add)
            osend[g, e] = own[g].astype(bf16)
            ro_copy(g, e).start()

        seen_slab(g, e, act)

    def cr_copy(k, from_offset):
        src = pgs.at[:, span(rem4(roll + steps[k]), 64), :]
        return rcopy(src, rec_r.at[rem4(roll + from_offset)], s_c.at[0, k], r_c.at[0, k], roll_dev(steps[k]))

    def cy_copy(k, from_offset):
        src = src_y.at[rem4(y + steps[k])]
        return rcopy(src, rec_y.at[rem4(y + from_offset)], s_c.at[1, k], r_c.at[1, k], y_dev(steps[k]))

    def cx_copy(k, from_offset):
        src = src_x.at[rem4(x + steps[k])]
        return rcopy(src, rec_x.at[rem4(x + from_offset)], s_c.at[2, k], r_c.at[2, k], x_dev(steps[k]))

    sum_copies = (cr_copy, cy_copy, cx_copy)

    def sum_start(stage):
        for k in range(3):
            sum_copies[stage](k, 0).start()

    def sum_wait(stage):
        for k in range(3):
            sum_copies[stage](k, 4 - steps[k]).wait_recv()

    def total4(ref):
        return (ref[0].astype(f32) + ref[1].astype(f32)) + (ref[2].astype(f32) + ref[3].astype(f32))

    @pl.loop(0, 10)
    def _(i):
        g = lax.rem(i, 2)
        kind = lax.div(i, 2)
        e = jnp.where(kind == 1, 2, jnp.where(kind == 2, 1, jnp.where(kind == 3, 3, 0)))
        none_seen = (g == 0) & (e > 0) & (y + e < 4)

        @pl.when(i == 5)
        def _():
            sum_wait(0)
            total_r = total4(rec_r)
            for r in range(4):
                rows = [total_r[:, t * 16 + r * 4 : t * 16 + r * 4 + 4, :] for t in range(4)]
                src_y[r] = jnp.concatenate(rows, axis=1).astype(bf16)
            sum_start(1)
            rec_y[y] = src_y[y]

        for h in range(2):

            @pl.when(i == 7 + h)
            def _():
                ro_start(h, 2)

        @pl.when(i == 9)
        def _():
            ro_start(0, 1)
            sum_wait(1)
            total_y = total4(rec_y)
            for r in range(4):
                rows = [total_y[:, t * 4 + r : t * 4 + r + 1, :] for t in range(4)]
                src_x[r] = jnp.concatenate(rows + rows, axis=1)
            sum_start(2)
            rec_x[x] = src_x[x]

        @pl.when(kind == 0)
        def _():
            bwd(g, 4, buf_b[g * 2], buf_b[g * 2 + 1], pp[g])
            pgs[g * 2] = acc[0, :PROMPT].astype(bf16)
            pgs[g * 2 + 1] = acc[1, :PROMPT].astype(bf16)

        @pl.when((kind != 0) & jnp.logical_not(none_seen))
        def _():
            bwd(g, e, kvb[g, e, 0], kvb[g, e, 1], pb[g, e])
            part[g, e] = acc[...].astype(bf16)

        @pl.when(kind == 4)
        def _():
            tot[g] = acc[:, :BLOCK, :]

        for h in range(2):
            for k, ahead in enumerate((None, 2, 1, 3, 0)):
                if ahead is not None:

                    @pl.when(i == 2 * k + h)
                    def _():
                        ri_start(h, ahead)

        @pl.when(i == 1)
        def _():
            sum_start(0)
            rec_r[roll] = pgs[:, span(roll, 64), :]

    ro_start(1, 1)
    for g in range(2):
        ro_start(g, 3)

    @pl.loop(0, 2)
    def _(g):
        rounded = (dq_t[g] * SCALE).astype(bf16)
        for h in range(GROUP):
            head = dot_nt(eye(BLOCK), rounded[:, h * BLOCK : (h + 1) * BLOCK])
            qg_ref[:, span(g * GROUP + h, HD)] = head.astype(bf16)

    qg_done = pltpu.make_async_copy(qg_ref, qg_hbm, s_io.at[4])
    qg_done.start()

    for g in range(2):

        def add_inner(k):
            ri_copy(g, 0, k).wait_recv()
            tot[g] += irec[g, 0, k].astype(f32)

        ri_do(g, 0, False, add_inner)
        for e in (2, 1, 3):

            def add_outer():
                ro_copy(g, e).wait_recv()
                tot[g] += orec[g, e].astype(f32)

            pl.when(y < e)(add_outer) if g == 0 else add_outer()
        for kv in range(2):
            okv_ref[kv, :, g * HD : (g + 1) * HD] = tot[g, kv]
    okv_done = pltpu.make_async_copy(okv_ref, okv_hbm, s_io.at[5])
    okv_done.start()

    sum_wait(2)
    total_d = total4(rec_x)
    for g in range(2):
        for kv in range(2):
            opk_ref[kv, :, g * HD : (g + 1) * HD] = total_d[g * 2 + kv, 0:4, :]
    opk_done = pltpu.make_async_copy(opk_ref, opk_hbm, s_io.at[6])
    opk_done.start()

    for g in range(2):
        for e in range(4):
            inner_do(g, e, True, lambda k: inner_copy(g, e, k).wait_send())
            ri_do(g, e, True, lambda k: ri_copy(g, e, k).wait_send())
            if e > 0:
                seen_slab(g, e, lambda: ro_copy(g, e).wait_send())
        for k in range(3):
            pl.when(y + steps[k] < 4)(lambda: outer_copy(g, k).wait_send()) if g == 0 else outer_copy(g, k).wait_send()
    for k in range(3):
        for copy in prompt_copies + sum_copies:
            copy(k, 0).wait_send()
    out_done.wait()
    qg_done.wait()
    okv_done.wait()
    opk_done.wait()


def store_kernel(a, b, c, d, a_out, b_out, c_out, d_out, sems):
    pairs = ((a, a_out), (b, b_out), (c, c_out), (d, d_out))
    copies = [pltpu.make_async_copy(src, dst, sems.at[i]) for i, (src, dst) in enumerate(pairs)]
    for copy in copies:
        copy.start()
    for copy in copies:
        copy.wait()


def shards(prompt_kv, comp_q, comp_kv, out_grad, lengths):
    vmem = pl.BlockSpec(memory_space=pltpu.VMEM)
    anywhere = pl.BlockSpec(memory_space=pl.ANY)
    dma = pltpu.SemaphoreType.DMA
    width = comp_q.shape[2]
    out_shape = (
        jax.ShapeDtypeStruct((BLOCK, width), bf16),
        jax.ShapeDtypeStruct((BLOCK, width), bf16),
        jax.ShapeDtypeStruct((2, BLOCK, 2 * HD), f32),
        jax.ShapeDtypeStruct((2, 4, 2 * HD), f32),
    )
    results = pl.pallas_call(
        kernel,
        out_shape=out_shape,
        in_specs=[pl.BlockSpec(memory_space=pltpu.SMEM), vmem] + [anywhere] * 3,
        out_specs=[anywhere] * 4,
        scratch_shapes=[
            pltpu.VMEM((BLOCK, width), bf16),
            pltpu.VMEM((2, BLOCK, 2 * HD), bf16),
            pltpu.VMEM((BLOCK, width), bf16),
            pltpu.VMEM((BLOCK, width), bf16),
            pltpu.VMEM((BLOCK, width), bf16),
            pltpu.VMEM((2, BLOCK, 2 * HD), f32),
            pltpu.VMEM((2, 4, 2 * HD), f32),
            pltpu.VMEM((2, ROWS, HD), bf16),
            pltpu.VMEM((2, ROWS, HD), bf16),
            pltpu.VMEM((2, 4, 2, SLAB, HD), bf16),
            pltpu.VMEM((2, 4, SLAB, ROWS), bf16),
            pltpu.VMEM((2, PROMPT, ROWS), bf16),
            pltpu.VMEM((2, 5, 1, ROWS), f32),
            pltpu.VMEM((2, 1, ROWS), f32),
            pltpu.VMEM((2, 1, ROWS), f32),
            pltpu.VMEM((2, HD, ROWS), f32),
            pltpu.VMEM((2, HD, ROWS), f32),
            pltpu.VMEM((2, 1, ROWS), f32),
            pltpu.VMEM((2, SLAB, HD), f32),
            pltpu.VMEM((2, 4, 2, SLAB, HD), bf16),
            pltpu.VMEM((2, 2, BLOCK, HD), f32),
            pltpu.VMEM((2, 2, BLOCK, HD), f32),
            pltpu.VMEM((2, 4, 3, 2, BLOCK, HD), bf16),
            pltpu.VMEM((2, 4, 2, BLOCK, HD), bf16),
            pltpu.VMEM((2, 4, 2, BLOCK, HD), bf16),
            pltpu.VMEM((16 * 16, HD), f32),
            pltpu.VMEM((4, 4, 16, HD), bf16),
            pltpu.VMEM((4, PROMPT, HD), bf16),
            pltpu.VMEM((4, PROMPT, HD), bf16),
            pltpu.VMEM((4, 4, 64, HD), bf16),
            pltpu.VMEM((4, 4, 16, HD), bf16),
            pltpu.VMEM((4, 4, 16, HD), bf16),
            pltpu.VMEM((4, 4, 8, HD), f32),
            pltpu.VMEM((4, 4, 8, HD), f32),
        ]
        + ([dma((2, 4, 3))] * 2 + [dma((2, 3))] * 2)
        + ([dma((2, 4, 3))] * 2 + [dma((2, 4))] * 2)
        + [dma((4, 3))] * 2
        + [dma((3, 3))] * 2
        + [dma((7,))],
        compiler_params=pltpu.CompilerParams(
            collective_id=0, has_side_effects=True, vmem_limit_bytes=56 * 2**20
        ),
    )(lengths, prompt_kv[:, 0], comp_q[0], comp_kv[:, 0], out_grad[0])
    out, q_grad, own_grad, prompt_grad = pl.pallas_call(
        store_kernel,
        out_shape=out_shape,
        in_specs=[vmem] * 4,
        out_specs=[anywhere] * 4,
        scratch_shapes=[dma((4,))],
    )(*results)
    return out[None], q_grad[None], own_grad[:, None], prompt_grad


def solution(mesh):
    in_specs = (
        P(None, ("roll", "seq", "tp"), None),
        P("roll", "seq", "tp"),
        P(None, "roll", "seq", "tp"),
        P("roll", "seq", "tp"),
        P("roll"),
    )
    out_specs = (
        P("roll", "seq", "tp"),
        P("roll", "seq", "tp"),
        P(None, "roll", "seq", "tp"),
        P(None, ("roll", "seq"), "tp"),
    )
    return jax.shard_map(shards, mesh=mesh, in_specs=in_specs, out_specs=out_specs, check_vma=False)
```

```python
import math

import jax
import jax.numpy as jnp
from jax import lax
from jax.experimental import pallas as pl
from jax.experimental.pallas import tpu as pltpu
from jax.sharding import PartitionSpec as P

HD = 128
BLOCK = 128
GROUP = 8
ROWS = GROUP * BLOCK
SLAB = 4 * BLOCK
PROMPT = 256
SCALE = 1.0 / math.sqrt(HD)
LOG2_SCALE = SCALE * math.log2(math.e)
FLOOR = -1e30
f32 = jnp.float32
bf16 = jnp.bfloat16
MESH = pl.DeviceIdType.MESH


def dot_nt(a, b):
    return lax.dot_general(a, b, (((1,), (1,)), ((), ())), preferred_element_type=f32)


def dot_nn(a, b):
    return lax.dot_general(a, b, (((1,), (0,)), ((), ())), preferred_element_type=f32)


def eye(n):
    rows = lax.broadcasted_iota(jnp.int32, (n, n), 0)
    cols = lax.broadcasted_iota(jnp.int32, (n, n), 1)
    return jnp.where(rows == cols, 1.0, 0.0).astype(bf16)


def rem4(i):
    return lax.rem(i, 4)


def kernel(
    len_ref, pk_ref, q_hbm, kv_hbm, do_hbm,
    out_hbm, qg_hbm, okv_hbm, opk_hbm,
    q_ref, kv_ref, do_ref, out_ref, qg_ref, okv_ref, opk_ref,
    qs, dos, kvb, pb, pp, mc, mx, sm, o_t, dq_t, dl, acc,
    part, own, tot, irec, osend, orec,
    buf_s, src_t, rec_t, buf_b, pgs, rec_y, src_r, rec_r, src_x, rec_x,
    s_in, r_in, s_out, r_out, s_ri, r_ri, s_ro, r_ro,
    s_p, r_p, s_c, r_c, s_io,
):
    roll = lax.axis_index("roll")
    seq = lax.axis_index("seq")
    tp = lax.axis_index("tp")
    y = lax.div(seq, 4)
    x = rem4(seq)
    length = len_ref[0]
    steps = (1, 3, 2)

    def x_dev(d):
        return {"seq": y * 4 + rem4(x + d)}

    def y_dev(d):
        return {"seq": rem4(y + d) * 4 + x}

    def roll_dev(d):
        return {"roll": rem4(roll + d)}

    def tp_dev(d):
        return {"tp": rem4(tp + d)}

    def inner(g, d):
        return x_dev(d) if g == 0 else y_dev(d)

    def outer(g, d):
        return y_dev(d) if g == 0 else x_dev(d)

    def rcopy(src, dst, ssem, rsem, dev):
        return pltpu.make_async_remote_copy(
            src_ref=src, dst_ref=dst, send_sem=ssem, recv_sem=rsem, device_id=dev, device_id_type=MESH
        )

    def span(i, n):
        return pl.ds(pl.multiple_of(i * n, n), n)

    barrier = pltpu.get_barrier_semaphore()
    for line in (tp_dev, roll_dev, y_dev, x_dev):
        for d in (2, 1, 3):
            pl.semaphore_signal(barrier, inc=1, device_id=line(d), device_id_type=MESH)
    kv_in = pltpu.make_async_copy(kv_hbm, kv_ref, s_io.at[0])
    q_in = pltpu.make_async_copy(q_hbm, q_ref, s_io.at[1])
    do_in = pltpu.make_async_copy(do_hbm, do_ref, s_io.at[2])
    kv_in.start()
    q_in.start()
    do_in.start()

    prompt_row = pk_ref[...].astype(f32)
    pieces = [prompt_row[:, t * HD : (t + 1) * HD] for t in range(8)]
    buf_s[span(x, 16), :] = jnp.concatenate(pieces, axis=0)
    kv_in.wait()
    for g in range(2):
        for kv in range(2):
            kvb[g, 0, kv, :BLOCK, :] = kv_ref[kv, :, g * HD : (g + 1) * HD]

    for p in range(1, 4):

        @pl.when(y + p < 4)
        def _():
            kvb[1, :, :, p * BLOCK : (p + 1) * BLOCK, :] = jnp.zeros((4, 2, BLOCK, HD), bf16)

        @pl.when(x + p < 4)
        def _():
            kvb[0, 0, :, p * BLOCK : (p + 1) * BLOCK, :] = jnp.zeros((2, BLOCK, HD), bf16)

    pl.semaphore_wait(barrier, 12)

    def seen_slab(g, e, act):
        if g == 0 and e > 0:
            pl.when(y + e >= 4)(act)
        else:
            act()

    def outer_copy(g, k):
        d = steps[k]
        src = kvb.at[g, 0, :, :BLOCK, :]
        return rcopy(src, kvb.at[g, 4 - d, :, :BLOCK, :], s_out.at[g, k], r_out.at[g, k], outer(g, d))

    def outer_start(g, k):
        def act():
            outer_copy(g, k).start()

        pl.when(y + steps[k] < 4)(act) if g == 0 else act()

    def inner_copy(g, e, k):
        d = steps[k]
        src = kvb.at[g, e, :, :BLOCK, :]
        dst = kvb.at[g, e, :, (4 - d) * BLOCK : (5 - d) * BLOCK, :]
        return rcopy(src, dst, s_in.at[g, e, k], r_in.at[g, e, k], inner(g, d))

    def inner_do(g, e, sends, act):
        def each():
            for k in range(3):
                at = x if g == 0 else y
                if g == 0 and e > 0:
                    act(k)
                else:
                    pl.when(at + steps[k] < 4 if sends else at >= steps[k])(lambda: act(k))

        seen_slab(g, e, each)

    def inner_start(g, e):
        inner_do(g, e, True, lambda k: inner_copy(g, e, k).start())

    def inner_wait(g, e):
        inner_do(g, e, False, lambda k: inner_copy(g, e, k).wait_recv())

    def px_copy(k, from_offset):
        ref = buf_s.at[span(rem4(x + from_offset), 16), :]
        return rcopy(ref, ref, s_p.at[0, k], r_p.at[0, k], x_dev(steps[k]))

    def tp_copy(k, from_offset):
        dst = rec_t.at[rem4(tp + from_offset)]
        return rcopy(src_t.at[rem4(tp + steps[k])], dst, s_p.at[1, k], r_p.at[1, k], tp_dev(steps[k]))

    def roll_copy(k, from_offset):
        ref = buf_b.at[:, span(y * 4 + rem4(roll + from_offset), 16), :]
        return rcopy(ref, ref, s_p.at[2, k], r_p.at[2, k], roll_dev(steps[k]))

    def py_copy(k, from_offset):
        ref = buf_b.at[:, span(rem4(y + from_offset), 64), :]
        return rcopy(ref, ref, s_p.at[3, k], r_p.at[3, k], y_dev(steps[k]))

    prompt_copies = (px_copy, tp_copy, roll_copy, py_copy)

    def prompt_start(stage):
        for k in range(3):
            prompt_copies[stage](k, 0).start()

    def prompt_wait(stage):
        for k in range(3):
            prompt_copies[stage](k, 4 - steps[k]).wait_recv()

    for k in range(3):
        for g in range(2):
            outer_start(g, k)
    prompt_start(0)
    for g in range(2):
        inner_start(g, 0)

    q_in.wait()
    do_in.wait()
    live_rows = seq * BLOCK + lax.broadcasted_iota(jnp.int32, (BLOCK, HD), 0) < length
    for g in range(2):
        for h in range(GROUP):
            cols = slice((g * GROUP + h) * HD, (g * GROUP + h + 1) * HD)
            rows = slice(h * BLOCK, (h + 1) * BLOCK)
            qs[g, rows, :] = q_ref[:, cols]
            dos[g, rows, :] = jnp.where(live_rows, do_ref[:, cols].astype(f32), 0.0).astype(bf16)
    mx[...] = jnp.full(mx.shape, FLOOR, f32)
    sm[...] = jnp.zeros(sm.shape, f32)
    o_t[...] = jnp.zeros(o_t.shape, f32)
    dq_t[...] = jnp.zeros(dq_t.shape, f32)

    prompt_wait(0)
    for t in range(4):
        for j in range(4):
            rows = buf_s[pl.ds(t * 4 + j, 4, stride=16), :]
            src_t[t, j] = jnp.concatenate([rows, rows], axis=0)
    prompt_start(1)
    rec_t[tp] = src_t[tp]
    def pass_on(k):
        for g in range(2):
            e = 4 - steps[k]
            seen_slab(g, e, lambda: outer_copy(g, k).wait_recv())
            inner_start(g, e)

    pass_on(0)
    pass_on(1)

    def fwd(g, c, k, v, p_ref, mask):
        n = k.shape[0]
        v_t = dot_nt(eye(HD), v).astype(bf16)
        s = dot_nt(k, qs[g]) * LOG2_SCALE
        if mask is not None:
            s = jnp.where(mask(n), s, FLOOR)
        m_old = mx[g]
        m_new = jnp.maximum(m_old, jnp.max(s, axis=0, keepdims=True))
        p = jnp.exp2(s - m_new)
        alpha = jnp.exp2(m_old - m_new)
        mx[g] = m_new
        mc[g, c] = m_new
        sm[g] = sm[g] * alpha + jnp.sum(p, axis=0, keepdims=True)
        rounded = p.astype(bf16)
        p_ref[...] = rounded
        o_t[g] = o_t[g] * alpha + dot_nn(v_t, rounded)

    def fwd_slab(g, e):
        none_seen = (g == 0) & (e > 0) & (y + e < 4)
        all_seen = jnp.where(g == 0, y + e >= 4, (y == 3) & (x + e >= 4))

        def mask(n):
            row = lax.broadcasted_iota(jnp.int32, (n, 1), 0)
            block = lax.div(row, BLOCK)
            key_y = rem4(y + jnp.where(g == 0, e, block))
            key_x = rem4(x + jnp.where(g == 0, block, e))
            key_block = key_y * 4 + key_x
            key_pos = key_block * BLOCK + lax.rem(row, BLOCK)
            lane = lax.broadcasted_iota(jnp.int32, (1, ROWS), 1)
            return key_pos <= seq * BLOCK + lax.rem(lane, BLOCK)

        @pl.when(all_seen)
        def _():
            fwd(g, e, kvb[g, e, 0], kvb[g, e, 1], pb.at[g, e], None)

        @pl.when(jnp.logical_not(all_seen | none_seen))
        def _():
            fwd(g, e, kvb[g, e, 0], kvb[g, e, 1], pb.at[g, e], mask)

    @pl.loop(0, 10)
    def _(i):
        g = lax.rem(i, 2)
        kind = lax.div(i, 2)

        for h in range(2):
            for k, e in enumerate((0, 3, 1, 2)):

                @pl.when(i == 2 * k + h)
                def _():
                    inner_wait(h, e)

        @pl.when(i == 1)
        def _():
            pass_on(2)
            prompt_wait(1)
            for j in range(4):
                rows = [rec_t[t, j, 0:4, :] for t in range(4)]
                buf_b[j, span(y * 4 + roll, 16), :] = jnp.concatenate(rows, axis=0).astype(bf16)
            prompt_start(2)

        @pl.when(i == 4)
        def _():
            prompt_wait(2)
            prompt_start(3)

        @pl.when(i == 8)
        def _():
            prompt_wait(3)

        @pl.when(kind == 4)
        def _():
            fwd(g, 4, buf_b[g * 2], buf_b[g * 2 + 1], pp.at[g], None)

        @pl.when(kind != 4)
        def _():
            fwd_slab(g, jnp.where(kind == 1, 3, jnp.where(kind == 2, 1, jnp.where(kind == 3, 2, 0))))

    @pl.loop(0, 2)
    def _(g):
        inv = 1.0 / sm[g]
        mixed = o_t[g] * inv
        dl[g] = jnp.sum(dot_nt(eye(HD), dos[g]) * mixed, axis=0, keepdims=True)
        sm[g] = inv
        lane = lax.broadcasted_iota(jnp.int32, (1, ROWS), 1)
        live = seq * BLOCK + lax.rem(lane, BLOCK) < length
        rounded = jnp.where(live, mixed, 0.0).astype(bf16)
        for h in range(GROUP):
            head = dot_nt(eye(BLOCK), rounded[:, h * BLOCK : (h + 1) * BLOCK])
            out_ref[:, span(g * GROUP + h, HD)] = head.astype(bf16)

    out_done = pltpu.make_async_copy(out_ref, out_hbm, s_io.at[3])
    out_done.start()

    def bwd(g, c, k, v, p):
        n = k.shape[0]
        k_t = dot_nt(eye(HD), k).astype(bf16)
        factor = jnp.exp2(mc[g, c] - mx[g]) * sm[g]
        dp = dot_nt(v, dos[g])
        w = p.astype(f32) * factor
        ds = (w * (dp - dl[g])).astype(bf16)
        acc[1, :n] = dot_nn(w.astype(bf16), dos[g])
        acc[0, :n] = dot_nn(ds, qs[g]) * SCALE
        dq_t[g] += dot_nn(k_t, ds)

    def ri_copy(g, e, k):
        d = steps[k]
        src = part.at[g, e, :, d * BLOCK : (d + 1) * BLOCK, :]
        return rcopy(src, irec.at[g, e, k], s_ri.at[g, e, k], r_ri.at[g, e, k], inner(g, d))

    def ri_do(g, e, sends, act):
        def each():
            for k in range(3):
                at = x if g == 0 else y
                if g == 0 and e > 0:
                    act(k)
                else:
                    pl.when(at + steps[k] >= 4 if sends else at < steps[k])(lambda: act(k))

        seen_slab(g, e, each)

    def ri_start(g, e):
        ri_do(g, e, True, lambda k: ri_copy(g, e, k).start())

    def ro_copy(g, e):
        return rcopy(osend.at[g, e], orec.at[g, e], s_ro.at[g, e], r_ro.at[g, e], outer(g, e))

    def ro_start(g, e):
        def act():
            own[g] = part[g, e, :, :BLOCK, :].astype(f32)

            def add(k):
                ri_copy(g, e, k).wait_recv()
                own[g] += irec[g, e, k].astype(f32)

            ri_do(g, e, False, add)
            osend[g, e] = own[g].astype(bf16)
            ro_copy(g, e).start()

        seen_slab(g, e, act)

    def cy_copy(k, from_offset):
        src = pgs.at[:, span(rem4(y + steps[k]), 64), :]
        return rcopy(src, rec_y.at[rem4(y + from_offset)], s_c.at[0, k], r_c.at[0, k], y_dev(steps[k]))

    def cr_copy(k, from_offset):
        src = src_r.at[:, span(rem4(roll + steps[k]), 16), :]
        return rcopy(src, rec_r.at[rem4(roll + from_offset)], s_c.at[1, k], r_c.at[1, k], roll_dev(steps[k]))

    def cx_copy(k, from_offset):
        src = src_x.at[rem4(x + steps[k])]
        return rcopy(src, rec_x.at[rem4(x + from_offset)], s_c.at[2, k], r_c.at[2, k], x_dev(steps[k]))

    sum_copies = (cy_copy, cr_copy, cx_copy)

    def sum_start(stage):
        for k in range(3):
            sum_copies[stage](k, 0).start()

    def sum_wait(stage):
        for k in range(3):
            sum_copies[stage](k, 4 - steps[k]).wait_recv()

    def total4(ref):
        return (ref[0].astype(f32) + ref[1].astype(f32)) + (ref[2].astype(f32) + ref[3].astype(f32))

    @pl.loop(0, 10)
    def _(i):
        g = lax.rem(i, 2)
        kind = lax.div(i, 2)
        e = jnp.where(kind == 1, 2, jnp.where(kind == 2, 1, jnp.where(kind == 3, 3, 0)))
        none_seen = (g == 0) & (e > 0) & (y + e < 4)

        @pl.when(i == 5)
        def _():
            sum_wait(0)
            src_r[...] = total4(rec_y).astype(bf16)
            sum_start(1)
            rec_r[roll] = src_r[:, span(roll, 16), :]

        for h in range(2):

            @pl.when(i == 7 + h)
            def _():
                ro_start(h, 2)

        @pl.when(i == 9)
        def _():
            ro_start(0, 1)
            sum_wait(1)
            total_r = total4(rec_r)
            for r in range(4):
                rows = [total_r[:, t * 4 + r : t * 4 + r + 1, :] for t in range(4)]
                src_x[r] = jnp.concatenate(rows + rows, axis=1)
            sum_start(2)
            rec_x[x] = src_x[x]

        @pl.when(kind == 0)
        def _():
            bwd(g, 4, buf_b[g * 2], buf_b[g * 2 + 1], pp[g])
            pgs[g * 2] = acc[0, :PROMPT].astype(bf16)
            pgs[g * 2 + 1] = acc[1, :PROMPT].astype(bf16)

        @pl.when((kind != 0) & jnp.logical_not(none_seen))
        def _():
            bwd(g, e, kvb[g, e, 0], kvb[g, e, 1], pb[g, e])
            part[g, e] = acc[...].astype(bf16)

        @pl.when(kind == 4)
        def _():
            tot[g] = acc[:, :BLOCK, :]

        for h in range(2):
            for k, ahead in enumerate((None, 2, 1, 3, 0)):
                if ahead is not None:

                    @pl.when(i == 2 * k + h)
                    def _():
                        ri_start(h, ahead)

        @pl.when(i == 1)
        def _():
            sum_start(0)
            rec_y[y] = pgs[:, span(y, 64), :]

    ro_start(1, 1)
    ro_start(0, 3)

    @pl.loop(0, 2)
    def _(g):
        rounded = (dq_t[g] * SCALE).astype(bf16)
        for h in range(GROUP):
            head = dot_nt(eye(BLOCK), rounded[:, h * BLOCK : (h + 1) * BLOCK])
            qg_ref[:, span(g * GROUP + h, HD)] = head.astype(bf16)

    ro_start(1, 3)
    qg_done = pltpu.make_async_copy(qg_ref, qg_hbm, s_io.at[4])
    qg_done.start()

    for g in range(2):

        def add_inner(k):
            ri_copy(g, 0, k).wait_recv()
            tot[g] += irec[g, 0, k].astype(f32)

        ri_do(g, 0, False, add_inner)
        for e in (2, 1, 3):

            def add_outer():
                ro_copy(g, e).wait_recv()
                tot[g] += orec[g, e].astype(f32)

            pl.when(y < e)(add_outer) if g == 0 else add_outer()
        for kv in range(2):
            okv_ref[kv, :, g * HD : (g + 1) * HD] = tot[g, kv]
    okv_done = pltpu.make_async_copy(okv_ref, okv_hbm, s_io.at[5])
    okv_done.start()

    sum_wait(2)
    total_d = total4(rec_x)
    for g in range(2):
        for kv in range(2):
            opk_ref[kv, :, g * HD : (g + 1) * HD] = total_d[g * 2 + kv, 0:4, :]
    opk_done = pltpu.make_async_copy(opk_ref, opk_hbm, s_io.at[6])
    opk_done.start()

    for g in range(2):
        for e in range(4):
            inner_do(g, e, True, lambda k: inner_copy(g, e, k).wait_send())
            ri_do(g, e, True, lambda k: ri_copy(g, e, k).wait_send())
            if e > 0:
                seen_slab(g, e, lambda: ro_copy(g, e).wait_send())
        for k in range(3):
            pl.when(y + steps[k] < 4)(lambda: outer_copy(g, k).wait_send()) if g == 0 else outer_copy(g, k).wait_send()
    for k in range(3):
        for copy in prompt_copies + sum_copies:
            copy(k, 0).wait_send()
    out_done.wait()
    qg_done.wait()
    okv_done.wait()
    opk_done.wait()


def store_kernel(a, b, c, d, a_out, b_out, c_out, d_out, sems):
    pairs = ((a, a_out), (b, b_out), (c, c_out), (d, d_out))
    copies = [pltpu.make_async_copy(src, dst, sems.at[i]) for i, (src, dst) in enumerate(pairs)]
    for copy in copies:
        copy.start()
    for copy in copies:
        copy.wait()


def shards(prompt_kv, comp_q, comp_kv, out_grad, lengths):
    vmem = pl.BlockSpec(memory_space=pltpu.VMEM)
    anywhere = pl.BlockSpec(memory_space=pl.ANY)
    dma = pltpu.SemaphoreType.DMA
    width = comp_q.shape[2]
    out_shape = (
        jax.ShapeDtypeStruct((BLOCK, width), bf16),
        jax.ShapeDtypeStruct((BLOCK, width), bf16),
        jax.ShapeDtypeStruct((2, BLOCK, 2 * HD), f32),
        jax.ShapeDtypeStruct((2, 4, 2 * HD), f32),
    )
    results = pl.pallas_call(
        kernel,
        out_shape=out_shape,
        in_specs=[pl.BlockSpec(memory_space=pltpu.SMEM), vmem] + [anywhere] * 3,
        out_specs=[anywhere] * 4,
        scratch_shapes=[
            pltpu.VMEM((BLOCK, width), bf16),
            pltpu.VMEM((2, BLOCK, 2 * HD), bf16),
            pltpu.VMEM((BLOCK, width), bf16),
            pltpu.VMEM((BLOCK, width), bf16),
            pltpu.VMEM((BLOCK, width), bf16),
            pltpu.VMEM((2, BLOCK, 2 * HD), f32),
            pltpu.VMEM((2, 4, 2 * HD), f32),
            pltpu.VMEM((2, ROWS, HD), bf16),
            pltpu.VMEM((2, ROWS, HD), bf16),
            pltpu.VMEM((2, 4, 2, SLAB, HD), bf16),
            pltpu.VMEM((2, 4, SLAB, ROWS), bf16),
            pltpu.VMEM((2, PROMPT, ROWS), bf16),
            pltpu.VMEM((2, 5, 1, ROWS), f32),
            pltpu.VMEM((2, 1, ROWS), f32),
            pltpu.VMEM((2, 1, ROWS), f32),
            pltpu.VMEM((2, HD, ROWS), f32),
            pltpu.VMEM((2, HD, ROWS), f32),
            pltpu.VMEM((2, 1, ROWS), f32),
            pltpu.VMEM((2, SLAB, HD), f32),
            pltpu.VMEM((2, 4, 2, SLAB, HD), bf16),
            pltpu.VMEM((2, 2, BLOCK, HD), f32),
            pltpu.VMEM((2, 2, BLOCK, HD), f32),
            pltpu.VMEM((2, 4, 3, 2, BLOCK, HD), bf16),
            pltpu.VMEM((2, 4, 2, BLOCK, HD), bf16),
            pltpu.VMEM((2, 4, 2, BLOCK, HD), bf16),
            pltpu.VMEM((4 * 16, HD), f32),
            pltpu.VMEM((4, 4, 8, HD), f32),
            pltpu.VMEM((4, 4, 8, HD), f32),
            pltpu.VMEM((4, PROMPT, HD), bf16),
            pltpu.VMEM((4, PROMPT, HD), bf16),
            pltpu.VMEM((4, 4, 64, HD), bf16),
            pltpu.VMEM((4, 64, HD), bf16),
            pltpu.VMEM((4, 4, 16, HD), bf16),
            pltpu.VMEM((4, 4, 8, HD), f32),
            pltpu.VMEM((4, 4, 8, HD), f32),
        ]
        + ([dma((2, 4, 3))] * 2 + [dma((2, 3))] * 2)
        + ([dma((2, 4, 3))] * 2 + [dma((2, 4))] * 2)
        + [dma((4, 3))] * 2
        + [dma((3, 3))] * 2
        + [dma((7,))],
        compiler_params=pltpu.CompilerParams(
            collective_id=0, has_side_effects=True, vmem_limit_bytes=56 * 2**20
        ),
    )(lengths, prompt_kv[:, 0], comp_q[0], comp_kv[:, 0], out_grad[0])
    out, q_grad, own_grad, prompt_grad = pl.pallas_call(
        store_kernel,
        out_shape=out_shape,
        in_specs=[vmem] * 4,
        out_specs=[anywhere] * 4,
        scratch_shapes=[dma((4,))],
    )(*results)
    return out[None], q_grad[None], own_grad[:, None], prompt_grad


def solution(mesh):
    in_specs = (
        P(None, ("roll", "seq", "tp"), None),
        P("roll", "seq", "tp"),
        P(None, "roll", "seq", "tp"),
        P("roll", "seq", "tp"),
        P("roll"),
    )
    out_specs = (
        P("roll", "seq", "tp"),
        P("roll", "seq", "tp"),
        P(None, "roll", "seq", "tp"),
        P(None, ("roll", "seq"), "tp"),
    )
    return jax.shard_map(shards, mesh=mesh, in_specs=in_specs, out_specs=out_specs, check_vma=False)
```

```python
import math

import jax
import jax.numpy as jnp
from jax import lax
from jax.experimental import pallas as pl
from jax.experimental.pallas import tpu as pltpu
from jax.sharding import PartitionSpec as P

HD = 128
BLOCK = 128
GROUP = 8
ROWS = GROUP * BLOCK
SLAB = 4 * BLOCK
PROMPT = 256
SCALE = 1.0 / math.sqrt(HD)
LOG2_SCALE = SCALE * math.log2(math.e)
FLOOR = -1e30
f32 = jnp.float32
bf16 = jnp.bfloat16
MESH = pl.DeviceIdType.MESH


def dot_nt(a, b):
    return lax.dot_general(a, b, (((1,), (1,)), ((), ())), preferred_element_type=f32)


def dot_nn(a, b):
    return lax.dot_general(a, b, (((1,), (0,)), ((), ())), preferred_element_type=f32)


def eye(n):
    rows = lax.broadcasted_iota(jnp.int32, (n, n), 0)
    cols = lax.broadcasted_iota(jnp.int32, (n, n), 1)
    return jnp.where(rows == cols, 1.0, 0.0).astype(bf16)


def rem4(i):
    return lax.rem(i, 4)


def kernel(
    len_ref, pk_ref, q_hbm, kv_hbm, do_hbm,
    out_hbm, qg_hbm, okv_hbm, opk_hbm,
    q_ref, kv_ref, do_ref, out_ref, qg_ref, okv_ref, opk_ref,
    qs, dos, kvb, pb, pp, mc, mx, sm, o_t, dq_t, dl, do_t,
    part, own, tot, irec, osend, orec,
    buf_s, src_t, rec_t, buf_b, pgs, rec_y, src_r, rec_r, src_x, rec_x,
    s_in, r_in, s_out, r_out, s_ri, r_ri, s_ro, r_ro,
    s_p, r_p, s_c, r_c, s_io,
):
    roll = lax.axis_index("roll")
    seq = lax.axis_index("seq")
    tp = lax.axis_index("tp")
    y = lax.div(seq, 4)
    x = rem4(seq)
    length = len_ref[0]
    steps = (1, 3, 2)

    def x_dev(d):
        return {"seq": y * 4 + rem4(x + d)}

    def y_dev(d):
        return {"seq": rem4(y + d) * 4 + x}

    def roll_dev(d):
        return {"roll": rem4(roll + d)}

    def tp_dev(d):
        return {"tp": rem4(tp + d)}

    def inner(g, d):
        return x_dev(d) if g == 0 else y_dev(d)

    def outer(g, d):
        return y_dev(d) if g == 0 else x_dev(d)

    def rcopy(src, dst, ssem, rsem, dev):
        return pltpu.make_async_remote_copy(
            src_ref=src, dst_ref=dst, send_sem=ssem, recv_sem=rsem, device_id=dev, device_id_type=MESH
        )

    def span(i, n):
        return pl.ds(pl.multiple_of(i * n, n), n)

    barrier = pltpu.get_barrier_semaphore()
    for line in (tp_dev, roll_dev, y_dev, x_dev):
        for d in (2, 1, 3):
            pl.semaphore_signal(barrier, inc=1, device_id=line(d), device_id_type=MESH)
    kv_in = pltpu.make_async_copy(kv_hbm, kv_ref, s_io.at[0])
    q_in = pltpu.make_async_copy(q_hbm, q_ref, s_io.at[1])
    do_in = pltpu.make_async_copy(do_hbm, do_ref, s_io.at[2])
    kv_in.start()
    q_in.start()
    do_in.start()

    prompt_row = pk_ref[...].astype(f32)
    pieces = [prompt_row[:, t * HD : (t + 1) * HD] for t in range(8)]
    buf_s[span(x, 16), :] = jnp.concatenate(pieces, axis=0)
    kv_in.wait()
    for g in range(2):
        for kv in range(2):
            kvb[g, 0, kv, :BLOCK, :] = kv_ref[kv, :, g * HD : (g + 1) * HD]

    for p in range(1, 4):

        @pl.when(y + p < 4)
        def _():
            kvb[1, :, :, p * BLOCK : (p + 1) * BLOCK, :] = jnp.zeros((4, 2, BLOCK, HD), bf16)

        @pl.when(x + p < 4)
        def _():
            kvb[0, 0, :, p * BLOCK : (p + 1) * BLOCK, :] = jnp.zeros((2, BLOCK, HD), bf16)

    pl.semaphore_wait(barrier, 12)

    def seen_slab(g, e, act):
        if g == 0 and e > 0:
            pl.when(y + e >= 4)(act)
        else:
            act()

    def outer_copy(g, k):
        d = steps[k]
        src = kvb.at[g, 0, :, :BLOCK, :]
        return rcopy(src, kvb.at[g, 4 - d, :, :BLOCK, :], s_out.at[g, k], r_out.at[g, k], outer(g, d))

    def outer_start(g, k):
        def act():
            outer_copy(g, k).start()

        pl.when(y + steps[k] < 4)(act) if g == 0 else act()

    def inner_copy(g, e, k):
        d = steps[k]
        src = kvb.at[g, e, :, :BLOCK, :]
        dst = kvb.at[g, e, :, (4 - d) * BLOCK : (5 - d) * BLOCK, :]
        return rcopy(src, dst, s_in.at[g, e, k], r_in.at[g, e, k], inner(g, d))

    def inner_do(g, e, sends, act):
        def each():
            for k in range(3):
                at = x if g == 0 else y
                if g == 0 and e > 0:
                    act(k)
                else:
                    pl.when(at + steps[k] < 4 if sends else at >= steps[k])(lambda: act(k))

        seen_slab(g, e, each)

    def inner_start(g, e):
        inner_do(g, e, True, lambda k: inner_copy(g, e, k).start())

    def inner_wait(g, e):
        inner_do(g, e, False, lambda k: inner_copy(g, e, k).wait_recv())

    def px_copy(k, from_offset):
        ref = buf_s.at[span(rem4(x + from_offset), 16), :]
        return rcopy(ref, ref, s_p.at[0, k], r_p.at[0, k], x_dev(steps[k]))

    def tp_copy(k, from_offset):
        dst = rec_t.at[rem4(tp + from_offset)]
        return rcopy(src_t.at[rem4(tp + steps[k])], dst, s_p.at[1, k], r_p.at[1, k], tp_dev(steps[k]))

    def roll_copy(k, from_offset):
        ref = buf_b.at[:, span(y * 4 + rem4(roll + from_offset), 16), :]
        return rcopy(ref, ref, s_p.at[2, k], r_p.at[2, k], roll_dev(steps[k]))

    def py_copy(k, from_offset):
        ref = buf_b.at[:, span(rem4(y + from_offset), 64), :]
        return rcopy(ref, ref, s_p.at[3, k], r_p.at[3, k], y_dev(steps[k]))

    prompt_copies = (px_copy, tp_copy, roll_copy, py_copy)

    def prompt_start(stage):
        for k in range(3):
            prompt_copies[stage](k, 0).start()

    def prompt_wait(stage):
        for k in range(3):
            prompt_copies[stage](k, 4 - steps[k]).wait_recv()

    for k in range(3):
        for g in range(2):
            outer_start(g, k)
    prompt_start(0)
    for g in range(2):
        inner_start(g, 0)

    q_in.wait()
    do_in.wait()
    live_rows = seq * BLOCK + lax.broadcasted_iota(jnp.int32, (BLOCK, HD), 0) < length
    for g in range(2):
        for h in range(GROUP):
            cols = slice((g * GROUP + h) * HD, (g * GROUP + h + 1) * HD)
            rows = slice(h * BLOCK, (h + 1) * BLOCK)
            qs[g, rows, :] = q_ref[:, cols]
            dos[g, rows, :] = jnp.where(live_rows, do_ref[:, cols].astype(f32), 0.0).astype(bf16)
    for g in range(2):
        do_t[g] = dot_nt(eye(HD), dos[g])
    mx[...] = jnp.full(mx.shape, FLOOR, f32)
    sm[...] = jnp.zeros(sm.shape, f32)
    o_t[...] = jnp.zeros(o_t.shape, f32)
    dq_t[...] = jnp.zeros(dq_t.shape, f32)

    prompt_wait(0)
    for t in range(4):
        for j in range(4):
            rows = buf_s[pl.ds(t * 4 + j, 4, stride=16), :]
            src_t[t, j] = jnp.concatenate([rows, rows], axis=0)
    prompt_start(1)
    rec_t[tp] = src_t[tp]
    def pass_on(k):
        for g in range(2):
            e = 4 - steps[k]
            seen_slab(g, e, lambda: outer_copy(g, k).wait_recv())
            inner_start(g, e)

    pass_on(0)
    pass_on(1)

    def fwd(g, c, k, v, p_ref, mask):
        n = k.shape[0]
        v_t = dot_nt(eye(HD), v).astype(bf16)
        s = dot_nt(k, qs[g]) * LOG2_SCALE
        if mask is not None:
            s = jnp.where(mask(n), s, FLOOR)
        m_old = mx[g]
        m_new = jnp.maximum(m_old, jnp.max(s, axis=0, keepdims=True))
        p = jnp.exp2(s - m_new)
        alpha = jnp.exp2(m_old - m_new)
        mx[g] = m_new
        mc[g, c] = m_new
        sm[g] = sm[g] * alpha + jnp.sum(p, axis=0, keepdims=True)
        rounded = p.astype(bf16)
        p_ref[...] = rounded
        o_t[g] = o_t[g] * alpha + dot_nn(v_t, rounded)

    def fwd_slab(g, e):
        none_seen = (g == 0) & (e > 0) & (y + e < 4)
        all_seen = jnp.where(g == 0, y + e >= 4, (y == 3) & (x + e >= 4))

        def mask(n):
            row = lax.broadcasted_iota(jnp.int32, (n, 1), 0)
            block = lax.div(row, BLOCK)
            key_y = rem4(y + jnp.where(g == 0, e, block))
            key_x = rem4(x + jnp.where(g == 0, block, e))
            key_block = key_y * 4 + key_x
            key_pos = key_block * BLOCK + lax.rem(row, BLOCK)
            lane = lax.broadcasted_iota(jnp.int32, (1, ROWS), 1)
            return key_pos <= seq * BLOCK + lax.rem(lane, BLOCK)

        @pl.when(all_seen)
        def _():
            fwd(g, e, kvb[g, e, 0], kvb[g, e, 1], pb.at[g, e], None)

        @pl.when(jnp.logical_not(all_seen | none_seen))
        def _():
            fwd(g, e, kvb[g, e, 0], kvb[g, e, 1], pb.at[g, e], mask)

    @pl.loop(0, 10)
    def _(i):
        g = lax.rem(i, 2)
        kind = lax.div(i, 2)

        for h in range(2):
            for k, e in enumerate((0, 3, 1, 2)):

                @pl.when(i == 2 * k + h)
                def _():
                    inner_wait(h, e)

        @pl.when(i == 1)
        def _():
            pass_on(2)
            prompt_wait(1)
            for j in range(4):
                rows = [rec_t[t, j, 0:4, :] for t in range(4)]
                buf_b[j, span(y * 4 + roll, 16), :] = jnp.concatenate(rows, axis=0).astype(bf16)
            prompt_start(2)

        @pl.when(i == 4)
        def _():
            prompt_wait(2)
            prompt_start(3)

        @pl.when(i == 8)
        def _():
            prompt_wait(3)

        @pl.when(kind == 4)
        def _():
            fwd(g, 4, buf_b[g * 2], buf_b[g * 2 + 1], pp.at[g], None)

        @pl.when(kind != 4)
        def _():
            fwd_slab(g, jnp.where(kind == 1, 3, jnp.where(kind == 2, 1, jnp.where(kind == 3, 2, 0))))

    @pl.loop(0, 2)
    def _(g):
        inv = 1.0 / sm[g]
        dl[g] = jnp.sum(do_t[g] * o_t[g], axis=0, keepdims=True) * inv
        sm[g] = inv

    def bwd(g, c, k, v, p):
        k_t = dot_nt(eye(HD), k).astype(bf16)
        factor = jnp.exp2(mc[g, c] - mx[g]) * sm[g]
        dp = dot_nt(v, dos[g])
        w = p.astype(f32) * factor
        ds = (w * (dp - dl[g])).astype(bf16)
        v_grad = dot_nn(w.astype(bf16), dos[g])
        k_grad = dot_nn(ds, qs[g]) * SCALE
        dq_t[g] += dot_nn(k_t, ds)
        return k_grad, v_grad

    def ri_copy(g, e, k):
        d = steps[k]
        src = part.at[g, e, :, d * BLOCK : (d + 1) * BLOCK, :]
        return rcopy(src, irec.at[g, e, k], s_ri.at[g, e, k], r_ri.at[g, e, k], inner(g, d))

    def ri_do(g, e, sends, act):
        def each():
            for k in range(3):
                at = x if g == 0 else y
                if g == 0 and e > 0:
                    act(k)
                else:
                    pl.when(at + steps[k] >= 4 if sends else at < steps[k])(lambda: act(k))

        seen_slab(g, e, each)

    def ri_start(g, e):
        ri_do(g, e, True, lambda k: ri_copy(g, e, k).start())

    def ro_copy(g, e):
        return rcopy(osend.at[g, e], orec.at[g, e], s_ro.at[g, e], r_ro.at[g, e], outer(g, e))

    def ro_start(g, e):
        def act():
            own[g] = part[g, e, :, :BLOCK, :].astype(f32)

            def add(k):
                ri_copy(g, e, k).wait_recv()
                own[g] += irec[g, e, k].astype(f32)

            ri_do(g, e, False, add)
            osend[g, e] = own[g].astype(bf16)
            ro_copy(g, e).start()

        seen_slab(g, e, act)

    def cy_copy(k, from_offset):
        src = pgs.at[:, span(rem4(y + steps[k]), 64), :]
        return rcopy(src, rec_y.at[rem4(y + from_offset)], s_c.at[0, k], r_c.at[0, k], y_dev(steps[k]))

    def cr_copy(k, from_offset):
        src = src_r.at[:, span(rem4(roll + steps[k]), 16), :]
        return rcopy(src, rec_r.at[rem4(roll + from_offset)], s_c.at[1, k], r_c.at[1, k], roll_dev(steps[k]))

    def cx_copy(k, from_offset):
        src = src_x.at[rem4(x + steps[k])]
        return rcopy(src, rec_x.at[rem4(x + from_offset)], s_c.at[2, k], r_c.at[2, k], x_dev(steps[k]))

    sum_copies = (cy_copy, cr_copy, cx_copy)

    def sum_start(stage):
        for k in range(3):
            sum_copies[stage](k, 0).start()

    def sum_wait(stage):
        for k in range(3):
            sum_copies[stage](k, 4 - steps[k]).wait_recv()

    def total4(ref):
        return (ref[0].astype(f32) + ref[1].astype(f32)) + (ref[2].astype(f32) + ref[3].astype(f32))

    @pl.loop(0, 10)
    def _(i):
        g = lax.rem(i, 2)
        kind = lax.div(i, 2)
        e = jnp.where(kind == 1, 2, jnp.where(kind == 2, 1, jnp.where(kind == 3, 3, 0)))
        none_seen = (g == 0) & (e > 0) & (y + e < 4)

        @pl.when(i == 5)
        def _():
            sum_wait(0)
            src_r[...] = total4(rec_y).astype(bf16)
            sum_start(1)
            rec_r[roll] = src_r[:, span(roll, 16), :]

        for h in range(2):

            @pl.when(i == 7 + h)
            def _():
                ro_start(h, 2)

        @pl.when(i == 9)
        def _():
            ro_start(0, 1)
            sum_wait(1)
            total_r = total4(rec_r)
            for r in range(4):
                rows = [total_r[:, t * 4 + r : t * 4 + r + 1, :] for t in range(4)]
                src_x[r] = jnp.concatenate(rows + rows, axis=1)
            sum_start(2)
            rec_x[x] = src_x[x]

        @pl.when(kind == 0)
        def _():
            for kv, grad in enumerate(bwd(g, 4, buf_b[g * 2], buf_b[g * 2 + 1], pp[g])):
                pgs[g * 2 + kv] = grad.astype(bf16)

        @pl.when((kind != 0) & jnp.logical_not(none_seen))
        def _():
            for kv, grad in enumerate(bwd(g, e, kvb[g, e, 0], kvb[g, e, 1], pb[g, e])):
                part[g, e, kv] = grad.astype(bf16)
                tot[g, kv] = grad[:BLOCK]

        for h in range(2):
            for k, ahead in enumerate((None, 2, 1, 3, 0)):
                if ahead is not None:

                    @pl.when(i == 2 * k + h)
                    def _():
                        ri_start(h, ahead)

        @pl.when(i == 1)
        def _():
            sum_start(0)
            rec_y[y] = pgs[:, span(y, 64), :]

    ro_start(1, 1)
    ro_start(0, 3)

    def store_heads(ref, g, transposed):
        rounded = transposed.astype(bf16)
        for h in range(GROUP):
            head = dot_nt(eye(BLOCK), rounded[:, h * BLOCK : (h + 1) * BLOCK])
            ref[:, span(g * GROUP + h, HD)] = head.astype(bf16)

    @pl.loop(0, 2)
    def _(g):
        lane = lax.broadcasted_iota(jnp.int32, (1, ROWS), 1)
        live = seq * BLOCK + lax.rem(lane, BLOCK) < length
        store_heads(out_ref, g, jnp.where(live, o_t[g] * sm[g], 0.0))
        store_heads(qg_ref, g, dq_t[g] * SCALE)

    out_done = pltpu.make_async_copy(out_ref, out_hbm, s_io.at[3])
    out_done.start()
    ro_start(1, 3)
    qg_done = pltpu.make_async_copy(qg_ref, qg_hbm, s_io.at[4])
    qg_done.start()

    for g in range(2):

        def add_inner(k):
            ri_copy(g, 0, k).wait_recv()
            tot[g] += irec[g, 0, k].astype(f32)

        ri_do(g, 0, False, add_inner)
        for e in (2, 1, 3):

            def add_outer():
                ro_copy(g, e).wait_recv()
                tot[g] += orec[g, e].astype(f32)

            pl.when(y < e)(add_outer) if g == 0 else add_outer()
        for kv in range(2):
            okv_ref[kv, :, g * HD : (g + 1) * HD] = tot[g, kv]
    okv_done = pltpu.make_async_copy(okv_ref, okv_hbm, s_io.at[5])
    okv_done.start()

    sum_wait(2)
    total_d = total4(rec_x)
    for g in range(2):
        for kv in range(2):
            opk_ref[kv, :, g * HD : (g + 1) * HD] = total_d[g * 2 + kv, 0:4, :]
    opk_done = pltpu.make_async_copy(opk_ref, opk_hbm, s_io.at[6])
    opk_done.start()

    for g in range(2):
        for e in range(4):
            inner_do(g, e, True, lambda k: inner_copy(g, e, k).wait_send())
            ri_do(g, e, True, lambda k: ri_copy(g, e, k).wait_send())
            if e > 0:
                seen_slab(g, e, lambda: ro_copy(g, e).wait_send())
        for k in range(3):
            pl.when(y + steps[k] < 4)(lambda: outer_copy(g, k).wait_send()) if g == 0 else outer_copy(g, k).wait_send()
    for k in range(3):
        for copy in prompt_copies + sum_copies:
            copy(k, 0).wait_send()
    out_done.wait()
    qg_done.wait()
    okv_done.wait()
    opk_done.wait()


def store_kernel(a, b, c, d, a_out, b_out, c_out, d_out, sems):
    pairs = ((a, a_out), (b, b_out), (c, c_out), (d, d_out))
    copies = [pltpu.make_async_copy(src, dst, sems.at[i]) for i, (src, dst) in enumerate(pairs)]
    for copy in copies:
        copy.start()
    for copy in copies:
        copy.wait()


def shards(prompt_kv, comp_q, comp_kv, out_grad, lengths):
    vmem = pl.BlockSpec(memory_space=pltpu.VMEM)
    anywhere = pl.BlockSpec(memory_space=pl.ANY)
    dma = pltpu.SemaphoreType.DMA
    width = comp_q.shape[2]
    out_shape = (
        jax.ShapeDtypeStruct((BLOCK, width), bf16),
        jax.ShapeDtypeStruct((BLOCK, width), bf16),
        jax.ShapeDtypeStruct((2, BLOCK, 2 * HD), f32),
        jax.ShapeDtypeStruct((2, 4, 2 * HD), f32),
    )
    results = pl.pallas_call(
        kernel,
        out_shape=out_shape,
        in_specs=[pl.BlockSpec(memory_space=pltpu.SMEM), vmem] + [anywhere] * 3,
        out_specs=[anywhere] * 4,
        scratch_shapes=[
            pltpu.VMEM((BLOCK, width), bf16),
            pltpu.VMEM((2, BLOCK, 2 * HD), bf16),
            pltpu.VMEM((BLOCK, width), bf16),
            pltpu.VMEM((BLOCK, width), bf16),
            pltpu.VMEM((BLOCK, width), bf16),
            pltpu.VMEM((2, BLOCK, 2 * HD), f32),
            pltpu.VMEM((2, 4, 2 * HD), f32),
            pltpu.VMEM((2, ROWS, HD), bf16),
            pltpu.VMEM((2, ROWS, HD), bf16),
            pltpu.VMEM((2, 4, 2, SLAB, HD), bf16),
            pltpu.VMEM((2, 4, SLAB, ROWS), bf16),
            pltpu.VMEM((2, PROMPT, ROWS), bf16),
            pltpu.VMEM((2, 5, 1, ROWS), f32),
            pltpu.VMEM((2, 1, ROWS), f32),
            pltpu.VMEM((2, 1, ROWS), f32),
            pltpu.VMEM((2, HD, ROWS), f32),
            pltpu.VMEM((2, HD, ROWS), f32),
            pltpu.VMEM((2, 1, ROWS), f32),
            pltpu.VMEM((2, HD, ROWS), f32),
            pltpu.VMEM((2, 4, 2, SLAB, HD), bf16),
            pltpu.VMEM((2, 2, BLOCK, HD), f32),
            pltpu.VMEM((2, 2, BLOCK, HD), f32),
            pltpu.VMEM((2, 4, 3, 2, BLOCK, HD), bf16),
            pltpu.VMEM((2, 4, 2, BLOCK, HD), bf16),
            pltpu.VMEM((2, 4, 2, BLOCK, HD), bf16),
            pltpu.VMEM((4 * 16, HD), f32),
            pltpu.VMEM((4, 4, 8, HD), f32),
            pltpu.VMEM((4, 4, 8, HD), f32),
            pltpu.VMEM((4, PROMPT, HD), bf16),
            pltpu.VMEM((4, PROMPT, HD), bf16),
            pltpu.VMEM((4, 4, 64, HD), bf16),
            pltpu.VMEM((4, 64, HD), bf16),
            pltpu.VMEM((4, 4, 16, HD), bf16),
            pltpu.VMEM((4, 4, 8, HD), f32),
            pltpu.VMEM((4, 4, 8, HD), f32),
        ]
        + ([dma((2, 4, 3))] * 2 + [dma((2, 3))] * 2)
        + ([dma((2, 4, 3))] * 2 + [dma((2, 4))] * 2)
        + [dma((4, 3))] * 2
        + [dma((3, 3))] * 2
        + [dma((7,))],
        compiler_params=pltpu.CompilerParams(
            collective_id=0, has_side_effects=True, vmem_limit_bytes=56 * 2**20
        ),
    )(lengths, prompt_kv[:, 0], comp_q[0], comp_kv[:, 0], out_grad[0])
    out, q_grad, own_grad, prompt_grad = pl.pallas_call(
        store_kernel,
        out_shape=out_shape,
        in_specs=[vmem] * 4,
        out_specs=[anywhere] * 4,
        scratch_shapes=[dma((4,))],
    )(*results)
    return out[None], q_grad[None], own_grad[:, None], prompt_grad


def solution(mesh):
    in_specs = (
        P(None, ("roll", "seq", "tp"), None),
        P("roll", "seq", "tp"),
        P(None, "roll", "seq", "tp"),
        P("roll", "seq", "tp"),
        P("roll"),
    )
    out_specs = (
        P("roll", "seq", "tp"),
        P("roll", "seq", "tp"),
        P(None, "roll", "seq", "tp"),
        P(None, ("roll", "seq"), "tp"),
    )
    return jax.shard_map(shards, mesh=mesh, in_specs=in_specs, out_specs=out_specs, check_vma=False)
```

```python
import math

import jax
import jax.numpy as jnp
from jax import lax
from jax.experimental import pallas as pl
from jax.experimental.pallas import tpu as pltpu
from jax.sharding import PartitionSpec as P

HD = 128
BLOCK = 128
GROUP = 8
ROWS = GROUP * BLOCK
SLAB = 4 * BLOCK
PROMPT = 256
SCALE = 1.0 / math.sqrt(HD)
LOG2_SCALE = SCALE * math.log2(math.e)
FLOOR = -1e30
f32 = jnp.float32
bf16 = jnp.bfloat16
MESH = pl.DeviceIdType.MESH


def dot_nt(a, b):
    return lax.dot_general(a, b, (((1,), (1,)), ((), ())), preferred_element_type=f32)


def dot_nn(a, b):
    return lax.dot_general(a, b, (((1,), (0,)), ((), ())), preferred_element_type=f32)


def eye(n):
    rows = lax.broadcasted_iota(jnp.int32, (n, n), 0)
    cols = lax.broadcasted_iota(jnp.int32, (n, n), 1)
    return jnp.where(rows == cols, 1.0, 0.0).astype(bf16)


def rem4(i):
    return lax.rem(i, 4)


def kernel(
    len_ref, pk_ref, q_hbm, kv_hbm, do_hbm,
    out_hbm, qg_hbm, okv_hbm, opk_hbm,
    q_ref, kv_ref, do_ref, out_ref, qg_ref, okv_ref, opk_ref,
    qs, dos, kvb, pb, pp, mc, mx, sm, o_t, dq_t, dl, do_t,
    part, own, tot, irec, osend, orec,
    buf_s, src_t, rec_t, buf_b, pgs, rec_y, src_r, rec_r, src_x, rec_x,
    s_in, r_in, s_out, r_out, s_ri, r_ri, s_ro, r_ro,
    s_p, r_p, s_c, r_c, s_io,
):
    roll = lax.axis_index("roll")
    seq = lax.axis_index("seq")
    tp = lax.axis_index("tp")
    y = lax.div(seq, 4)
    x = rem4(seq)
    length = len_ref[0]
    steps = (1, 3, 2)

    def x_dev(d):
        return {"seq": y * 4 + rem4(x + d)}

    def y_dev(d):
        return {"seq": rem4(y + d) * 4 + x}

    def roll_dev(d):
        return {"roll": rem4(roll + d)}

    def tp_dev(d):
        return {"tp": rem4(tp + d)}

    def inner(g, d):
        return x_dev(d) if g == 0 else y_dev(d)

    def outer(g, d):
        return y_dev(d) if g == 0 else x_dev(d)

    def rcopy(src, dst, ssem, rsem, dev):
        return pltpu.make_async_remote_copy(
            src_ref=src, dst_ref=dst, send_sem=ssem, recv_sem=rsem, device_id=dev, device_id_type=MESH
        )

    def span(i, n):
        return pl.ds(pl.multiple_of(i * n, n), n)

    barrier = pltpu.get_barrier_semaphore()
    for line in (tp_dev, roll_dev, y_dev, x_dev):
        for d in (2, 1, 3):
            pl.semaphore_signal(barrier, inc=1, device_id=line(d), device_id_type=MESH)
    kv_in = pltpu.make_async_copy(kv_hbm, kv_ref, s_io.at[0])
    q_in = pltpu.make_async_copy(q_hbm, q_ref, s_io.at[1])
    do_in = pltpu.make_async_copy(do_hbm, do_ref, s_io.at[2])
    kv_in.start()
    q_in.start()
    do_in.start()

    prompt_row = pk_ref[...].astype(f32)
    pieces = [prompt_row[:, t * HD : (t + 1) * HD] for t in range(8)]
    buf_s[span(x, 16), :] = jnp.concatenate(pieces, axis=0)
    kv_in.wait()
    for g in range(2):
        for kv in range(2):
            kvb[g, 0, kv, :BLOCK, :] = kv_ref[kv, :, g * HD : (g + 1) * HD]

    for p in range(1, 4):

        @pl.when(y + p < 4)
        def _():
            kvb[1, :, :, p * BLOCK : (p + 1) * BLOCK, :] = jnp.zeros((4, 2, BLOCK, HD), bf16)

        @pl.when(x + p < 4)
        def _():
            kvb[0, 0, :, p * BLOCK : (p + 1) * BLOCK, :] = jnp.zeros((2, BLOCK, HD), bf16)

        @pl.when((y == 3) & (x + p < 4))
        def _():
            kvb[1, p, :, :BLOCK, :] = jnp.zeros((2, BLOCK, HD), bf16)

    pl.semaphore_wait(barrier, 12)

    def seen_slab(g, e, act):
        if g == 0 and e > 0:
            pl.when(y + e >= 4)(act)
        else:
            act()

    def outer_copy(g, k):
        d = steps[k]
        src = kvb.at[g, 0, :, :BLOCK, :]
        return rcopy(src, kvb.at[g, 4 - d, :, :BLOCK, :], s_out.at[g, k], r_out.at[g, k], outer(g, d))

    def outer_sent(g, k, act):
        d = steps[k]
        pl.when(y + d < 4 if g == 0 else (y < 3) | (x + d < 4))(act)

    def outer_seen(g, k, act):
        d = steps[k]
        pl.when(y >= d if g == 0 else (y < 3) | (x >= d))(act)

    def sum_sent(g, e, act):
        pl.when(y + e >= 4 if g == 0 else (y < 3) | (x + e >= 4))(act)

    def sum_seen(g, e, act):
        pl.when(y < e if g == 0 else (y < 3) | (x < e))(act)

    def outer_start(g, k):
        outer_sent(g, k, lambda: outer_copy(g, k).start())

    def inner_copy(g, e, k):
        d = steps[k]
        src = kvb.at[g, e, :, :BLOCK, :]
        dst = kvb.at[g, e, :, (4 - d) * BLOCK : (5 - d) * BLOCK, :]
        return rcopy(src, dst, s_in.at[g, e, k], r_in.at[g, e, k], inner(g, d))

    def inner_do(g, e, sends, act):
        def each():
            for k in range(3):
                at = x if g == 0 else y
                if g == 0 and e > 0:
                    act(k)
                else:
                    pl.when(at + steps[k] < 4 if sends else at >= steps[k])(lambda: act(k))

        seen_slab(g, e, each)

    def inner_start(g, e):
        inner_do(g, e, True, lambda k: inner_copy(g, e, k).start())

    def inner_wait(g, e):
        inner_do(g, e, False, lambda k: inner_copy(g, e, k).wait_recv())

    def px_copy(k, from_offset):
        ref = buf_s.at[span(rem4(x + from_offset), 16), :]
        return rcopy(ref, ref, s_p.at[0, k], r_p.at[0, k], x_dev(steps[k]))

    def tp_copy(k, from_offset):
        dst = rec_t.at[rem4(tp + from_offset)]
        return rcopy(src_t.at[rem4(tp + steps[k])], dst, s_p.at[1, k], r_p.at[1, k], tp_dev(steps[k]))

    def roll_copy(k, from_offset):
        ref = buf_b.at[:, span(y * 4 + rem4(roll + from_offset), 16), :]
        return rcopy(ref, ref, s_p.at[2, k], r_p.at[2, k], roll_dev(steps[k]))

    def py_copy(k, from_offset):
        ref = buf_b.at[:, span(rem4(y + from_offset), 64), :]
        return rcopy(ref, ref, s_p.at[3, k], r_p.at[3, k], y_dev(steps[k]))

    prompt_copies = (px_copy, tp_copy, roll_copy, py_copy)

    def prompt_start(stage):
        for k in range(3):
            prompt_copies[stage](k, 0).start()

    def prompt_wait(stage):
        for k in range(3):
            prompt_copies[stage](k, 4 - steps[k]).wait_recv()

    prompt_start(0)
    for k in range(3):
        for g in range(2):
            outer_start(g, k)
    for g in range(2):
        inner_start(g, 0)

    q_in.wait()
    do_in.wait()
    live_rows = seq * BLOCK + lax.broadcasted_iota(jnp.int32, (BLOCK, HD), 0) < length
    for g in range(2):
        for h in range(GROUP):
            cols = slice((g * GROUP + h) * HD, (g * GROUP + h + 1) * HD)
            rows = slice(h * BLOCK, (h + 1) * BLOCK)
            qs[g, rows, :] = q_ref[:, cols]
            dos[g, rows, :] = jnp.where(live_rows, do_ref[:, cols].astype(f32), 0.0).astype(bf16)
    for g in range(2):
        do_t[g] = dot_nt(eye(HD), dos[g])
    mx[...] = jnp.full(mx.shape, FLOOR, f32)
    sm[...] = jnp.zeros(sm.shape, f32)
    o_t[...] = jnp.zeros(o_t.shape, f32)
    dq_t[...] = jnp.zeros(dq_t.shape, f32)

    prompt_wait(0)
    for t in range(4):
        for j in range(4):
            rows = buf_s[pl.ds(t * 4 + j, 4, stride=16), :]
            src_t[t, j] = jnp.concatenate([rows, rows], axis=0)
    prompt_start(1)
    rec_t[tp] = src_t[tp]
    def pass_on(k):
        for g in range(2):
            e = 4 - steps[k]
            outer_seen(g, k, lambda: outer_copy(g, k).wait_recv())
            inner_start(g, e)

    pass_on(0)
    pass_on(1)

    def fwd(g, c, k, v, p_ref, mask):
        n = k.shape[0]
        v_t = dot_nt(eye(HD), v).astype(bf16)
        s = dot_nt(k, qs[g]) * LOG2_SCALE
        if mask is not None:
            s = jnp.where(mask(n), s, FLOOR)
        m_old = mx[g]
        m_new = jnp.maximum(m_old, jnp.max(s, axis=0, keepdims=True))
        p = jnp.exp2(s - m_new)
        alpha = jnp.exp2(m_old - m_new)
        mx[g] = m_new
        mc[g, c] = m_new
        sm[g] = sm[g] * alpha + jnp.sum(p, axis=0, keepdims=True)
        rounded = p.astype(bf16)
        p_ref[...] = rounded
        o_t[g] = o_t[g] * alpha + dot_nn(v_t, rounded)

    def fwd_slab(g, e):
        none_seen = (g == 0) & (e > 0) & (y + e < 4)
        all_seen = jnp.where(g == 0, y + e >= 4, (y == 3) & (x + e >= 4))

        def mask(n):
            row = lax.broadcasted_iota(jnp.int32, (n, 1), 0)
            block = lax.div(row, BLOCK)
            key_y = rem4(y + jnp.where(g == 0, e, block))
            key_x = rem4(x + jnp.where(g == 0, block, e))
            key_block = key_y * 4 + key_x
            key_pos = key_block * BLOCK + lax.rem(row, BLOCK)
            lane = lax.broadcasted_iota(jnp.int32, (1, ROWS), 1)
            return key_pos <= seq * BLOCK + lax.rem(lane, BLOCK)

        @pl.when(all_seen)
        def _():
            fwd(g, e, kvb[g, e, 0], kvb[g, e, 1], pb.at[g, e], None)

        @pl.when(jnp.logical_not(all_seen | none_seen))
        def _():
            fwd(g, e, kvb[g, e, 0], kvb[g, e, 1], pb.at[g, e], mask)

    @pl.loop(0, 10)
    def _(i):
        g = lax.rem(i, 2)
        kind = lax.div(i, 2)

        for h in range(2):
            for k, e in enumerate((0, 3, 1, 2)):

                @pl.when(i == 2 * k + h)
                def _():
                    inner_wait(h, e)

        @pl.when(i == 1)
        def _():
            pass_on(2)
            prompt_wait(1)
            for j in range(4):
                rows = [rec_t[t, j, 0:4, :] for t in range(4)]
                buf_b[j, span(y * 4 + roll, 16), :] = jnp.concatenate(rows, axis=0).astype(bf16)
            prompt_start(2)

        @pl.when(i == 4)
        def _():
            prompt_wait(2)
            prompt_start(3)

        @pl.when(i == 8)
        def _():
            prompt_wait(3)

        @pl.when(kind == 4)
        def _():
            fwd(g, 4, buf_b[g * 2], buf_b[g * 2 + 1], pp.at[g], None)

        @pl.when(kind != 4)
        def _():
            fwd_slab(g, jnp.where(kind == 1, 3, jnp.where(kind == 2, 1, jnp.where(kind == 3, 2, 0))))

    @pl.loop(0, 2)
    def _(g):
        inv = 1.0 / sm[g]
        dl[g] = jnp.sum(do_t[g] * o_t[g], axis=0, keepdims=True) * inv
        sm[g] = inv

    def bwd(g, c, k, v, p):
        k_t = dot_nt(eye(HD), k).astype(bf16)
        factor = jnp.exp2(mc[g, c] - mx[g]) * sm[g]
        dp = dot_nt(v, dos[g])
        w = p.astype(f32) * factor
        ds = (w * (dp - dl[g])).astype(bf16)
        v_grad = dot_nn(w.astype(bf16), dos[g])
        k_grad = dot_nn(ds, qs[g]) * SCALE
        dq_t[g] += dot_nn(k_t, ds)
        return k_grad, v_grad

    def ri_copy(g, e, k):
        d = steps[k]
        src = part.at[g, e, :, d * BLOCK : (d + 1) * BLOCK, :]
        return rcopy(src, irec.at[g, e, k], s_ri.at[g, e, k], r_ri.at[g, e, k], inner(g, d))

    def ri_do(g, e, sends, act):
        def each():
            for k in range(3):
                at = x if g == 0 else y
                if g == 0 and e > 0:
                    act(k)
                else:
                    pl.when(at + steps[k] >= 4 if sends else at < steps[k])(lambda: act(k))

        seen_slab(g, e, each)

    def ri_start(g, e):
        ri_do(g, e, True, lambda k: ri_copy(g, e, k).start())

    def ro_copy(g, e):
        return rcopy(osend.at[g, e], orec.at[g, e], s_ro.at[g, e], r_ro.at[g, e], outer(g, e))

    def ro_start(g, e):
        def act():
            own[g] = part[g, e, :, :BLOCK, :].astype(f32)

            def add(k):
                ri_copy(g, e, k).wait_recv()
                own[g] += irec[g, e, k].astype(f32)

            ri_do(g, e, False, add)
            osend[g, e] = own[g].astype(bf16)
            ro_copy(g, e).start()

        sum_sent(g, e, act)

    def cy_copy(k, from_offset):
        src = pgs.at[:, span(rem4(y + steps[k]), 64), :]
        return rcopy(src, rec_y.at[rem4(y + from_offset)], s_c.at[0, k], r_c.at[0, k], y_dev(steps[k]))

    def cr_copy(k, from_offset):
        src = src_r.at[:, span(rem4(roll + steps[k]), 16), :]
        return rcopy(src, rec_r.at[rem4(roll + from_offset)], s_c.at[1, k], r_c.at[1, k], roll_dev(steps[k]))

    def cx_copy(k, from_offset):
        src = src_x.at[rem4(x + steps[k])]
        return rcopy(src, rec_x.at[rem4(x + from_offset)], s_c.at[2, k], r_c.at[2, k], x_dev(steps[k]))

    sum_copies = (cy_copy, cr_copy, cx_copy)

    def sum_start(stage):
        for k in range(3):
            sum_copies[stage](k, 0).start()

    def sum_wait(stage):
        for k in range(3):
            sum_copies[stage](k, 4 - steps[k]).wait_recv()

    def total4(ref):
        return (ref[0].astype(f32) + ref[1].astype(f32)) + (ref[2].astype(f32) + ref[3].astype(f32))

    @pl.loop(0, 10)
    def _(i):
        g = lax.rem(i, 2)
        kind = lax.div(i, 2)
        e = jnp.where(kind == 1, 2, jnp.where(kind == 2, 1, jnp.where(kind == 3, 3, 0)))
        none_seen = (g == 0) & (e > 0) & (y + e < 4)

        @pl.when(i == 5)
        def _():
            sum_wait(0)
            src_r[...] = total4(rec_y).astype(bf16)
            sum_start(1)
            rec_r[roll] = src_r[:, span(roll, 16), :]

        for h in range(2):

            @pl.when(i == 7 + h)
            def _():
                ro_start(h, 2)

        @pl.when(i == 9)
        def _():
            ro_start(0, 1)
            sum_wait(1)
            total_r = total4(rec_r)
            for r in range(4):
                rows = [total_r[:, t * 4 + r : t * 4 + r + 1, :] for t in range(4)]
                src_x[r] = jnp.concatenate(rows + rows, axis=1)
            sum_start(2)
            rec_x[x] = src_x[x]

        @pl.when(kind == 0)
        def _():
            for kv, grad in enumerate(bwd(g, 4, buf_b[g * 2], buf_b[g * 2 + 1], pp[g])):
                pgs[g * 2 + kv] = grad.astype(bf16)

        @pl.when((kind != 0) & jnp.logical_not(none_seen))
        def _():
            for kv, grad in enumerate(bwd(g, e, kvb[g, e, 0], kvb[g, e, 1], pb[g, e])):
                part[g, e, kv] = grad.astype(bf16)
                tot[g, kv] = grad[:BLOCK]

        for h in range(2):
            for k, ahead in enumerate((None, 2, 1, 3, 0)):
                if ahead is not None:

                    @pl.when(i == 2 * k + h)
                    def _():
                        ri_start(h, ahead)

        @pl.when(i == 1)
        def _():
            sum_start(0)
            rec_y[y] = pgs[:, span(y, 64), :]

    ro_start(1, 1)
    ro_start(0, 3)

    def store_heads(ref, g, transposed):
        rounded = transposed.astype(bf16)
        for h in range(GROUP):
            head = dot_nt(eye(BLOCK), rounded[:, h * BLOCK : (h + 1) * BLOCK])
            ref[:, span(g * GROUP + h, HD)] = head.astype(bf16)

    @pl.loop(0, 2)
    def _(g):
        lane = lax.broadcasted_iota(jnp.int32, (1, ROWS), 1)
        live = seq * BLOCK + lax.rem(lane, BLOCK) < length
        store_heads(out_ref, g, jnp.where(live, o_t[g] * sm[g], 0.0))
        store_heads(qg_ref, g, dq_t[g] * SCALE)

    out_done = pltpu.make_async_copy(out_ref, out_hbm, s_io.at[3])
    out_done.start()
    ro_start(1, 3)
    qg_done = pltpu.make_async_copy(qg_ref, qg_hbm, s_io.at[4])
    qg_done.start()

    for g in range(2):

        def add_inner(k):
            ri_copy(g, 0, k).wait_recv()
            tot[g] += irec[g, 0, k].astype(f32)

        ri_do(g, 0, False, add_inner)
        for e in (2, 1, 3):

            def add_outer():
                ro_copy(g, e).wait_recv()
                tot[g] += orec[g, e].astype(f32)

            sum_seen(g, e, add_outer)
        for kv in range(2):
            okv_ref[kv, :, g * HD : (g + 1) * HD] = tot[g, kv]
    okv_done = pltpu.make_async_copy(okv_ref, okv_hbm, s_io.at[5])
    okv_done.start()

    sum_wait(2)
    total_d = total4(rec_x)
    for g in range(2):
        for kv in range(2):
            opk_ref[kv, :, g * HD : (g + 1) * HD] = total_d[g * 2 + kv, 0:4, :]
    opk_done = pltpu.make_async_copy(opk_ref, opk_hbm, s_io.at[6])
    opk_done.start()

    for g in range(2):
        for e in range(4):
            inner_do(g, e, True, lambda k: inner_copy(g, e, k).wait_send())
            ri_do(g, e, True, lambda k: ri_copy(g, e, k).wait_send())
            if e > 0:
                sum_sent(g, e, lambda: ro_copy(g, e).wait_send())
        for k in range(3):
            outer_sent(g, k, lambda: outer_copy(g, k).wait_send())
    for k in range(3):
        for copy in prompt_copies + sum_copies:
            copy(k, 0).wait_send()
    out_done.wait()
    qg_done.wait()
    okv_done.wait()
    opk_done.wait()


def store_kernel(a, b, c, d, a_out, b_out, c_out, d_out, sems):
    pairs = ((a, a_out), (b, b_out), (c, c_out), (d, d_out))
    copies = [pltpu.make_async_copy(src, dst, sems.at[i]) for i, (src, dst) in enumerate(pairs)]
    for copy in copies:
        copy.start()
    for copy in copies:
        copy.wait()


def shards(prompt_kv, comp_q, comp_kv, out_grad, lengths):
    vmem = pl.BlockSpec(memory_space=pltpu.VMEM)
    anywhere = pl.BlockSpec(memory_space=pl.ANY)
    dma = pltpu.SemaphoreType.DMA
    width = comp_q.shape[2]
    out_shape = (
        jax.ShapeDtypeStruct((BLOCK, width), bf16),
        jax.ShapeDtypeStruct((BLOCK, width), bf16),
        jax.ShapeDtypeStruct((2, BLOCK, 2 * HD), f32),
        jax.ShapeDtypeStruct((2, 4, 2 * HD), f32),
    )
    results = pl.pallas_call(
        kernel,
        out_shape=out_shape,
        in_specs=[pl.BlockSpec(memory_space=pltpu.SMEM), vmem] + [anywhere] * 3,
        out_specs=[anywhere] * 4,
        scratch_shapes=[
            pltpu.VMEM((BLOCK, width), bf16),
            pltpu.VMEM((2, BLOCK, 2 * HD), bf16),
            pltpu.VMEM((BLOCK, width), bf16),
            pltpu.VMEM((BLOCK, width), bf16),
            pltpu.VMEM((BLOCK, width), bf16),
            pltpu.VMEM((2, BLOCK, 2 * HD), f32),
            pltpu.VMEM((2, 4, 2 * HD), f32),
            pltpu.VMEM((2, ROWS, HD), bf16),
            pltpu.VMEM((2, ROWS, HD), bf16),
            pltpu.VMEM((2, 4, 2, SLAB, HD), bf16),
            pltpu.VMEM((2, 4, SLAB, ROWS), bf16),
            pltpu.VMEM((2, PROMPT, ROWS), bf16),
            pltpu.VMEM((2, 5, 1, ROWS), f32),
            pltpu.VMEM((2, 1, ROWS), f32),
            pltpu.VMEM((2, 1, ROWS), f32),
            pltpu.VMEM((2, HD, ROWS), f32),
            pltpu.VMEM((2, HD, ROWS), f32),
            pltpu.VMEM((2, 1, ROWS), f32),
            pltpu.VMEM((2, HD, ROWS), f32),
            pltpu.VMEM((2, 4, 2, SLAB, HD), bf16),
            pltpu.VMEM((2, 2, BLOCK, HD), f32),
            pltpu.VMEM((2, 2, BLOCK, HD), f32),
            pltpu.VMEM((2, 4, 3, 2, BLOCK, HD), bf16),
            pltpu.VMEM((2, 4, 2, BLOCK, HD), bf16),
            pltpu.VMEM((2, 4, 2, BLOCK, HD), bf16),
            pltpu.VMEM((4 * 16, HD), f32),
            pltpu.VMEM((4, 4, 8, HD), f32),
            pltpu.VMEM((4, 4, 8, HD), f32),
            pltpu.VMEM((4, PROMPT, HD), bf16),
            pltpu.VMEM((4, PROMPT, HD), bf16),
            pltpu.VMEM((4, 4, 64, HD), bf16),
            pltpu.VMEM((4, 64, HD), bf16),
            pltpu.VMEM((4, 4, 16, HD), bf16),
            pltpu.VMEM((4, 4, 8, HD), f32),
            pltpu.VMEM((4, 4, 8, HD), f32),
        ]
        + ([dma((2, 4, 3))] * 2 + [dma((2, 3))] * 2)
        + ([dma((2, 4, 3))] * 2 + [dma((2, 4))] * 2)
        + [dma((4, 3))] * 2
        + [dma((3, 3))] * 2
        + [dma((7,))],
        compiler_params=pltpu.CompilerParams(
            collective_id=0, has_side_effects=True, vmem_limit_bytes=56 * 2**20
        ),
    )(lengths, prompt_kv[:, 0], comp_q[0], comp_kv[:, 0], out_grad[0])
    out, q_grad, own_grad, prompt_grad = pl.pallas_call(
        store_kernel,
        out_shape=out_shape,
        in_specs=[vmem] * 4,
        out_specs=[anywhere] * 4,
        scratch_shapes=[dma((4,))],
    )(*results)
    return out[None], q_grad[None], own_grad[:, None], prompt_grad


def solution(mesh):
    in_specs = (
        P(None, ("roll", "seq", "tp"), None),
        P("roll", "seq", "tp"),
        P(None, "roll", "seq", "tp"),
        P("roll", "seq", "tp"),
        P("roll"),
    )
    out_specs = (
        P("roll", "seq", "tp"),
        P("roll", "seq", "tp"),
        P(None, "roll", "seq", "tp"),
        P(None, ("roll", "seq"), "tp"),
    )
    return jax.shard_map(shards, mesh=mesh, in_specs=in_specs, out_specs=out_specs, check_vma=False)
```

```python
import math

import jax
import jax.numpy as jnp
from jax import lax
from jax.experimental import pallas as pl
from jax.experimental.pallas import tpu as pltpu
from jax.sharding import PartitionSpec as P

HD = 128
BLOCK = 128
GROUP = 8
ROWS = GROUP * BLOCK
SLAB = 4 * BLOCK
PROMPT = 256
SCALE = 1.0 / math.sqrt(HD)
LOG2_SCALE = SCALE * math.log2(math.e)
FLOOR = -1e30
f32 = jnp.float32
bf16 = jnp.bfloat16
MESH = pl.DeviceIdType.MESH


def dot_nt(a, b):
    return lax.dot_general(a, b, (((1,), (1,)), ((), ())), preferred_element_type=f32)


def dot_nn(a, b):
    return lax.dot_general(a, b, (((1,), (0,)), ((), ())), preferred_element_type=f32)


def eye(n):
    rows = lax.broadcasted_iota(jnp.int32, (n, n), 0)
    cols = lax.broadcasted_iota(jnp.int32, (n, n), 1)
    return jnp.where(rows == cols, 1.0, 0.0).astype(bf16)


def rem4(i):
    return lax.rem(i, 4)


def kernel(
    len_ref, pk_ref, q_hbm, kv_hbm, do_hbm,
    out_hbm, qg_hbm, okv_hbm, opk_hbm,
    q_ref, kv_ref, do_ref, out_ref, qg_ref, okv_ref, opk_ref,
    qs, dos, kvb, pb, pp, mc, mx, sm, o_t, dq_t, dl, do_t,
    part, own, tot, irec, osend, orec,
    buf_s, src_t, rec_t, buf_b, pgs, rec_y, src_r, rec_r, src_x, rec_x,
    s_in, r_in, s_out, r_out, s_ri, r_ri, s_ro, r_ro,
    s_p, r_p, s_c, r_c, s_io,
):
    roll = lax.axis_index("roll")
    seq = lax.axis_index("seq")
    tp = lax.axis_index("tp")
    y = lax.div(seq, 4)
    x = rem4(seq)
    length = len_ref[0]
    steps = (1, 3, 2)

    def x_dev(d):
        return {"seq": y * 4 + rem4(x + d)}

    def y_dev(d):
        return {"seq": rem4(y + d) * 4 + x}

    def roll_dev(d):
        return {"roll": rem4(roll + d)}

    def tp_dev(d):
        return {"tp": rem4(tp + d)}

    def inner(g, d):
        return x_dev(d) if g == 0 else y_dev(d)

    def outer(g, d):
        return y_dev(d) if g == 0 else x_dev(d)

    def rcopy(src, dst, ssem, rsem, dev):
        return pltpu.make_async_remote_copy(
            src_ref=src, dst_ref=dst, send_sem=ssem, recv_sem=rsem, device_id=dev, device_id_type=MESH
        )

    def span(i, n):
        return pl.ds(pl.multiple_of(i * n, n), n)

    barrier = pltpu.get_barrier_semaphore()
    for line in (tp_dev, roll_dev, y_dev, x_dev):
        for d in (2, 1, 3):
            pl.semaphore_signal(barrier, inc=1, device_id=line(d), device_id_type=MESH)
    kv_in = pltpu.make_async_copy(kv_hbm, kv_ref, s_io.at[0])
    q_in = pltpu.make_async_copy(q_hbm, q_ref, s_io.at[1])
    do_in = pltpu.make_async_copy(do_hbm, do_ref, s_io.at[2])
    kv_in.start()
    q_in.start()
    do_in.start()

    prompt_row = pk_ref[...].astype(f32)
    pieces = [prompt_row[:, t * HD : (t + 1) * HD] for t in range(8)]
    buf_s[span(x, 16), :] = jnp.concatenate(pieces, axis=0)
    kv_in.wait()
    for g in range(2):
        for kv in range(2):
            kvb[g, 0, kv, :BLOCK, :] = kv_ref[kv, :, g * HD : (g + 1) * HD]

    for p in range(1, 4):

        @pl.when(y + p < 4)
        def _():
            kvb[1, :, :, p * BLOCK : (p + 1) * BLOCK, :] = jnp.zeros((4, 2, BLOCK, HD), bf16)

        @pl.when(x + p < 4)
        def _():
            kvb[0, 0, :, p * BLOCK : (p + 1) * BLOCK, :] = jnp.zeros((2, BLOCK, HD), bf16)

        @pl.when((y == 3) & (x + p < 4))
        def _():
            kvb[1, p, :, :BLOCK, :] = jnp.zeros((2, BLOCK, HD), bf16)

    pl.semaphore_wait(barrier, 12)

    def seen_slab(g, e, act):
        if g == 0 and e > 0:
            pl.when(y + e >= 4)(act)
        else:
            act()

    def outer_copy(g, k):
        d = steps[k]
        src = kvb.at[g, 0, :, :BLOCK, :]
        return rcopy(src, kvb.at[g, 4 - d, :, :BLOCK, :], s_out.at[g, k], r_out.at[g, k], outer(g, d))

    def outer_sent(g, k, act):
        d = steps[k]
        pl.when(y + d < 4 if g == 0 else (y < 3) | (x + d < 4))(act)

    def outer_seen(g, k, act):
        d = steps[k]
        pl.when(y >= d if g == 0 else (y < 3) | (x >= d))(act)

    def sum_sent(g, e, act):
        pl.when(y + e >= 4 if g == 0 else (y < 3) | (x + e >= 4))(act)

    def sum_seen(g, e, act):
        pl.when(y < e if g == 0 else (y < 3) | (x < e))(act)

    def outer_start(g, k):
        outer_sent(g, k, lambda: outer_copy(g, k).start())

    def inner_copy(g, e, k):
        d = steps[k]
        src = kvb.at[g, e, :, :BLOCK, :]
        dst = kvb.at[g, e, :, (4 - d) * BLOCK : (5 - d) * BLOCK, :]
        return rcopy(src, dst, s_in.at[g, e, k], r_in.at[g, e, k], inner(g, d))

    def inner_do(g, e, sends, act):
        def each():
            for k in range(3):
                at = x if g == 0 else y
                if g == 0 and e > 0:
                    act(k)
                else:
                    pl.when(at + steps[k] < 4 if sends else at >= steps[k])(lambda: act(k))

        seen_slab(g, e, each)

    def inner_start(g, e):
        inner_do(g, e, True, lambda k: inner_copy(g, e, k).start())

    def inner_wait(g, e):
        inner_do(g, e, False, lambda k: inner_copy(g, e, k).wait_recv())

    def px_copy(k, from_offset):
        ref = buf_s.at[span(rem4(x + from_offset), 16), :]
        return rcopy(ref, ref, s_p.at[0, k], r_p.at[0, k], x_dev(steps[k]))

    def tp_copy(k, from_offset):
        dst = rec_t.at[rem4(tp + from_offset)]
        return rcopy(src_t.at[rem4(tp + steps[k])], dst, s_p.at[1, k], r_p.at[1, k], tp_dev(steps[k]))

    def roll_copy(k, from_offset):
        ref = buf_b.at[:, span(y * 4 + rem4(roll + from_offset), 16), :]
        return rcopy(ref, ref, s_p.at[2, k], r_p.at[2, k], roll_dev(steps[k]))

    def py_copy(k, from_offset):
        ref = buf_b.at[:, span(rem4(y + from_offset), 64), :]
        return rcopy(ref, ref, s_p.at[3, k], r_p.at[3, k], y_dev(steps[k]))

    prompt_copies = (px_copy, tp_copy, roll_copy, py_copy)

    def prompt_start(stage):
        for k in range(3):
            prompt_copies[stage](k, 0).start()

    def prompt_wait(stage):
        for k in range(3):
            prompt_copies[stage](k, 4 - steps[k]).wait_recv()

    prompt_start(0)
    for k in range(3):
        for g in range(2):
            outer_start(g, k)
    for g in range(2):
        inner_start(g, 0)

    q_in.wait()
    do_in.wait()
    live_rows = seq * BLOCK + lax.broadcasted_iota(jnp.int32, (BLOCK, HD), 0) < length
    for g in range(2):
        for h in range(GROUP):
            cols = slice((g * GROUP + h) * HD, (g * GROUP + h + 1) * HD)
            rows = slice(h * BLOCK, (h + 1) * BLOCK)
            qs[g, rows, :] = q_ref[:, cols]
            dos[g, rows, :] = jnp.where(live_rows, do_ref[:, cols].astype(f32), 0.0).astype(bf16)
    for g in range(2):
        do_t[g] = dot_nt(eye(HD), dos[g])
    mx[...] = jnp.full(mx.shape, FLOOR, f32)
    sm[...] = jnp.zeros(sm.shape, f32)
    o_t[...] = jnp.zeros(o_t.shape, f32)
    dq_t[...] = jnp.zeros(dq_t.shape, f32)

    prompt_wait(0)
    for t in range(4):
        for j in range(4):
            rows = buf_s[pl.ds(t * 4 + j, 4, stride=16), :]
            src_t[t, j] = jnp.concatenate([rows, rows], axis=0)
    prompt_start(1)
    rec_t[tp] = src_t[tp]
    def pass_on(k):
        for g in range(2):
            e = 4 - steps[k]
            outer_seen(g, k, lambda: outer_copy(g, k).wait_recv())
            inner_start(g, e)

    pass_on(0)
    pass_on(1)

    def fwd(g, c, k, v, p_ref, mask):
        n = k.shape[0]
        v_t = dot_nt(eye(HD), v).astype(bf16)
        s = dot_nt(k, qs[g]) * LOG2_SCALE
        if mask is not None:
            s = jnp.where(mask(n), s, FLOOR)
        m_old = mx[g]
        m_new = jnp.maximum(m_old, jnp.max(s, axis=0, keepdims=True))
        p = jnp.exp2(s - m_new)
        alpha = jnp.exp2(m_old - m_new)
        mx[g] = m_new
        mc[g, c] = m_new
        sm[g] = sm[g] * alpha + jnp.sum(p, axis=0, keepdims=True)
        rounded = p.astype(bf16)
        p_ref[...] = rounded
        o_t[g] = o_t[g] * alpha + dot_nn(v_t, rounded)

    def fwd_slab(g, e):
        none_seen = (g == 0) & (e > 0) & (y + e < 4)
        all_seen = jnp.where(g == 0, y + e >= 4, (y == 3) & (x + e >= 4))

        def mask(n):
            row = lax.broadcasted_iota(jnp.int32, (n, 1), 0)
            block = lax.div(row, BLOCK)
            key_y = rem4(y + jnp.where(g == 0, e, block))
            key_x = rem4(x + jnp.where(g == 0, block, e))
            key_block = key_y * 4 + key_x
            key_pos = key_block * BLOCK + lax.rem(row, BLOCK)
            lane = lax.broadcasted_iota(jnp.int32, (1, ROWS), 1)
            return key_pos <= seq * BLOCK + lax.rem(lane, BLOCK)

        @pl.when(all_seen)
        def _():
            fwd(g, e, kvb[g, e, 0], kvb[g, e, 1], pb.at[g, e], None)

        @pl.when(jnp.logical_not(all_seen | none_seen))
        def _():
            fwd(g, e, kvb[g, e, 0], kvb[g, e, 1], pb.at[g, e], mask)

    @pl.loop(0, 10)
    def _(i):
        g = lax.rem(i, 2)
        kind = lax.div(i, 2)

        for h in range(2):
            for k, e in enumerate((0, 3, 1, 2)):

                @pl.when(i == 2 * k + h)
                def _():
                    inner_wait(h, e)

        @pl.when(i == 1)
        def _():
            pass_on(2)
            prompt_wait(1)
            for j in range(4):
                rows = [rec_t[t, j, 0:4, :] for t in range(4)]
                buf_b[j, span(y * 4 + roll, 16), :] = jnp.concatenate(rows, axis=0).astype(bf16)
            prompt_start(2)

        @pl.when(i == 3)
        def _():
            prompt_wait(2)
            prompt_start(3)

        @pl.when(i == 8)
        def _():
            prompt_wait(3)

        @pl.when(kind == 4)
        def _():
            fwd(g, 4, buf_b[g * 2], buf_b[g * 2 + 1], pp.at[g], None)

        @pl.when(kind != 4)
        def _():
            fwd_slab(g, jnp.where(kind == 1, 3, jnp.where(kind == 2, 1, jnp.where(kind == 3, 2, 0))))

    @pl.loop(0, 2)
    def _(g):
        inv = 1.0 / sm[g]
        dl[g] = jnp.sum(do_t[g] * o_t[g], axis=0, keepdims=True) * inv
        sm[g] = inv

    def bwd(g, c, k, v, p):
        k_t = dot_nt(eye(HD), k).astype(bf16)
        factor = jnp.exp2(mc[g, c] - mx[g]) * sm[g]
        dp = dot_nt(v, dos[g])
        w = p.astype(f32) * factor
        ds = (w * (dp - dl[g])).astype(bf16)
        v_grad = dot_nn(w.astype(bf16), dos[g])
        k_grad = dot_nn(ds, qs[g]) * SCALE
        dq_t[g] += dot_nn(k_t, ds)
        return k_grad, v_grad

    def ri_copy(g, e, k):
        d = steps[k]
        src = part.at[g, e, :, d * BLOCK : (d + 1) * BLOCK, :]
        return rcopy(src, irec.at[g, e, k], s_ri.at[g, e, k], r_ri.at[g, e, k], inner(g, d))

    def ri_do(g, e, sends, act):
        def each():
            for k in range(3):
                at = x if g == 0 else y
                if g == 0 and e > 0:
                    act(k)
                else:
                    pl.when(at + steps[k] >= 4 if sends else at < steps[k])(lambda: act(k))

        seen_slab(g, e, each)

    def ri_start(g, e):
        ri_do(g, e, True, lambda k: ri_copy(g, e, k).start())

    def ro_copy(g, e):
        return rcopy(osend.at[g, e], orec.at[g, e], s_ro.at[g, e], r_ro.at[g, e], outer(g, e))

    def ro_start(g, e):
        def act():
            own[g] = part[g, e, :, :BLOCK, :].astype(f32)

            def add(k):
                ri_copy(g, e, k).wait_recv()
                own[g] += irec[g, e, k].astype(f32)

            ri_do(g, e, False, add)
            osend[g, e] = own[g].astype(bf16)
            ro_copy(g, e).start()

        sum_sent(g, e, act)

    def cy_copy(k, from_offset):
        src = pgs.at[:, span(rem4(y + steps[k]), 64), :]
        return rcopy(src, rec_y.at[rem4(y + from_offset)], s_c.at[0, k], r_c.at[0, k], y_dev(steps[k]))

    def cr_copy(k, from_offset):
        src = src_r.at[:, span(rem4(roll + steps[k]), 16), :]
        return rcopy(src, rec_r.at[rem4(roll + from_offset)], s_c.at[1, k], r_c.at[1, k], roll_dev(steps[k]))

    def cx_copy(k, from_offset):
        src = src_x.at[rem4(x + steps[k])]
        return rcopy(src, rec_x.at[rem4(x + from_offset)], s_c.at[2, k], r_c.at[2, k], x_dev(steps[k]))

    sum_copies = (cy_copy, cr_copy, cx_copy)

    def sum_start(stage):
        for k in range(3):
            sum_copies[stage](k, 0).start()

    def sum_wait(stage):
        for k in range(3):
            sum_copies[stage](k, 4 - steps[k]).wait_recv()

    def total4(ref):
        return (ref[0].astype(f32) + ref[1].astype(f32)) + (ref[2].astype(f32) + ref[3].astype(f32))

    @pl.loop(0, 10)
    def _(i):
        g = lax.rem(i, 2)
        kind = lax.div(i, 2)
        e = jnp.where(kind == 1, 2, jnp.where(kind == 2, 1, jnp.where(kind == 3, 3, 0)))
        none_seen = (g == 0) & (e > 0) & (y + e < 4)

        @pl.when(i == 5)
        def _():
            sum_wait(0)
            src_r[...] = total4(rec_y).astype(bf16)
            sum_start(1)
            rec_r[roll] = src_r[:, span(roll, 16), :]

        for h in range(2):

            @pl.when(i == 7 + h)
            def _():
                ro_start(h, 2)

        @pl.when(i == 9)
        def _():
            ro_start(0, 1)
            sum_wait(1)
            total_r = total4(rec_r)
            for r in range(4):
                rows = [total_r[:, t * 4 + r : t * 4 + r + 1, :] for t in range(4)]
                src_x[r] = jnp.concatenate(rows + rows, axis=1)
            sum_start(2)
            rec_x[x] = src_x[x]

        @pl.when(kind == 0)
        def _():
            for kv, grad in enumerate(bwd(g, 4, buf_b[g * 2], buf_b[g * 2 + 1], pp[g])):
                pgs[g * 2 + kv] = grad.astype(bf16)

        @pl.when((kind != 0) & jnp.logical_not(none_seen))
        def _():
            for kv, grad in enumerate(bwd(g, e, kvb[g, e, 0], kvb[g, e, 1], pb[g, e])):
                part[g, e, kv] = grad.astype(bf16)
                tot[g, kv] = grad[:BLOCK]

        for h in range(2):
            for k, ahead in enumerate((None, 2, 1, 3, 0)):
                if ahead is not None:

                    @pl.when(i == 2 * k + h)
                    def _():
                        ri_start(h, ahead)

        @pl.when(i == 1)
        def _():
            sum_start(0)
            rec_y[y] = pgs[:, span(y, 64), :]

    ro_start(1, 1)
    ro_start(0, 3)

    def store_heads(ref, g, transposed):
        rounded = transposed.astype(bf16)
        for h in range(GROUP):
            head = dot_nt(eye(BLOCK), rounded[:, h * BLOCK : (h + 1) * BLOCK])
            ref[:, span(g * GROUP + h, HD)] = head.astype(bf16)

    @pl.loop(0, 2)
    def _(g):
        lane = lax.broadcasted_iota(jnp.int32, (1, ROWS), 1)
        live = seq * BLOCK + lax.rem(lane, BLOCK) < length
        store_heads(out_ref, g, jnp.where(live, o_t[g] * sm[g], 0.0))
        store_heads(qg_ref, g, dq_t[g] * SCALE)

    out_done = pltpu.make_async_copy(out_ref, out_hbm, s_io.at[3])
    out_done.start()
    ro_start(1, 3)
    qg_done = pltpu.make_async_copy(qg_ref, qg_hbm, s_io.at[4])
    qg_done.start()

    for g in range(2):

        def add_inner(k):
            ri_copy(g, 0, k).wait_recv()
            tot[g] += irec[g, 0, k].astype(f32)

        ri_do(g, 0, False, add_inner)
        for e in (2, 1, 3):

            def add_outer():
                ro_copy(g, e).wait_recv()
                tot[g] += orec[g, e].astype(f32)

            sum_seen(g, e, add_outer)
        for kv in range(2):
            okv_ref[kv, :, g * HD : (g + 1) * HD] = tot[g, kv]
    okv_done = pltpu.make_async_copy(okv_ref, okv_hbm, s_io.at[5])
    okv_done.start()

    sum_wait(2)
    total_d = total4(rec_x)
    for g in range(2):
        for kv in range(2):
            opk_ref[kv, :, g * HD : (g + 1) * HD] = total_d[g * 2 + kv, 0:4, :]
    opk_done = pltpu.make_async_copy(opk_ref, opk_hbm, s_io.at[6])
    opk_done.start()

    for g in range(2):
        for e in range(4):
            inner_do(g, e, True, lambda k: inner_copy(g, e, k).wait_send())
            ri_do(g, e, True, lambda k: ri_copy(g, e, k).wait_send())
            if e > 0:
                sum_sent(g, e, lambda: ro_copy(g, e).wait_send())
        for k in range(3):
            outer_sent(g, k, lambda: outer_copy(g, k).wait_send())
    for k in range(3):
        for copy in prompt_copies + sum_copies:
            copy(k, 0).wait_send()
    out_done.wait()
    qg_done.wait()
    okv_done.wait()
    opk_done.wait()


def store_kernel(a, b, c, d, a_out, b_out, c_out, d_out, sems):
    pairs = ((a, a_out), (b, b_out), (c, c_out), (d, d_out))
    copies = [pltpu.make_async_copy(src, dst, sems.at[i]) for i, (src, dst) in enumerate(pairs)]
    for copy in copies:
        copy.start()
    for copy in copies:
        copy.wait()


def shards(prompt_kv, comp_q, comp_kv, out_grad, lengths):
    vmem = pl.BlockSpec(memory_space=pltpu.VMEM)
    anywhere = pl.BlockSpec(memory_space=pl.ANY)
    dma = pltpu.SemaphoreType.DMA
    width = comp_q.shape[2]
    out_shape = (
        jax.ShapeDtypeStruct((BLOCK, width), bf16),
        jax.ShapeDtypeStruct((BLOCK, width), bf16),
        jax.ShapeDtypeStruct((2, BLOCK, 2 * HD), f32),
        jax.ShapeDtypeStruct((2, 4, 2 * HD), f32),
    )
    results = pl.pallas_call(
        kernel,
        out_shape=out_shape,
        in_specs=[pl.BlockSpec(memory_space=pltpu.SMEM), vmem] + [anywhere] * 3,
        out_specs=[anywhere] * 4,
        scratch_shapes=[
            pltpu.VMEM((BLOCK, width), bf16),
            pltpu.VMEM((2, BLOCK, 2 * HD), bf16),
            pltpu.VMEM((BLOCK, width), bf16),
            pltpu.VMEM((BLOCK, width), bf16),
            pltpu.VMEM((BLOCK, width), bf16),
            pltpu.VMEM((2, BLOCK, 2 * HD), f32),
            pltpu.VMEM((2, 4, 2 * HD), f32),
            pltpu.VMEM((2, ROWS, HD), bf16),
            pltpu.VMEM((2, ROWS, HD), bf16),
            pltpu.VMEM((2, 4, 2, SLAB, HD), bf16),
            pltpu.VMEM((2, 4, SLAB, ROWS), bf16),
            pltpu.VMEM((2, PROMPT, ROWS), bf16),
            pltpu.VMEM((2, 5, 1, ROWS), f32),
            pltpu.VMEM((2, 1, ROWS), f32),
            pltpu.VMEM((2, 1, ROWS), f32),
            pltpu.VMEM((2, HD, ROWS), f32),
            pltpu.VMEM((2, HD, ROWS), f32),
            pltpu.VMEM((2, 1, ROWS), f32),
            pltpu.VMEM((2, HD, ROWS), f32),
            pltpu.VMEM((2, 4, 2, SLAB, HD), bf16),
            pltpu.VMEM((2, 2, BLOCK, HD), f32),
            pltpu.VMEM((2, 2, BLOCK, HD), f32),
            pltpu.VMEM((2, 4, 3, 2, BLOCK, HD), bf16),
            pltpu.VMEM((2, 4, 2, BLOCK, HD), bf16),
            pltpu.VMEM((2, 4, 2, BLOCK, HD), bf16),
            pltpu.VMEM((4 * 16, HD), f32),
            pltpu.VMEM((4, 4, 8, HD), f32),
            pltpu.VMEM((4, 4, 8, HD), f32),
            pltpu.VMEM((4, PROMPT, HD), bf16),
            pltpu.VMEM((4, PROMPT, HD), bf16),
            pltpu.VMEM((4, 4, 64, HD), bf16),
            pltpu.VMEM((4, 64, HD), bf16),
            pltpu.VMEM((4, 4, 16, HD), bf16),
            pltpu.VMEM((4, 4, 8, HD), f32),
            pltpu.VMEM((4, 4, 8, HD), f32),
        ]
        + ([dma((2, 4, 3))] * 2 + [dma((2, 3))] * 2)
        + ([dma((2, 4, 3))] * 2 + [dma((2, 4))] * 2)
        + [dma((4, 3))] * 2
        + [dma((3, 3))] * 2
        + [dma((7,))],
        compiler_params=pltpu.CompilerParams(
            collective_id=0, has_side_effects=True, vmem_limit_bytes=56 * 2**20
        ),
    )(lengths, prompt_kv[:, 0], comp_q[0], comp_kv[:, 0], out_grad[0])
    out, q_grad, own_grad, prompt_grad = pl.pallas_call(
        store_kernel,
        out_shape=out_shape,
        in_specs=[vmem] * 4,
        out_specs=[anywhere] * 4,
        scratch_shapes=[dma((4,))],
    )(*results)
    return out[None], q_grad[None], own_grad[:, None], prompt_grad


def solution(mesh):
    in_specs = (
        P(None, ("roll", "seq", "tp"), None),
        P("roll", "seq", "tp"),
        P(None, "roll", "seq", "tp"),
        P("roll", "seq", "tp"),
        P("roll"),
    )
    out_specs = (
        P("roll", "seq", "tp"),
        P("roll", "seq", "tp"),
        P(None, "roll", "seq", "tp"),
        P(None, ("roll", "seq"), "tp"),
    )
    return jax.shard_map(shards, mesh=mesh, in_specs=in_specs, out_specs=out_specs, check_vma=False)
```
